32 devices in a mesh: kpt: 2 (over y), dom: 8 (over z, x), band: 2 (over core).
Axes of the slice: x: 2, y: 2, z: 4, core: 2. Of those that a mesh axis runs over, the one named last changes fastest.
Arguments:
- wavefunctions: bfloat16 [65536, 256], P(('kpt', 'dom'), 'band'), parts along dimension 0, may hold values from -40 to 40
- bounds: float32 [4], P('kpt'), parts along dimension 0, may hold values from 0.5 to 23, as said below
- cell_matrix: bfloat16 [512, 512], replicated, may hold values from -1 to 4, as said below
- cell_scale: float32 [128], P('dom'), may hold values from 0.5 to 6
- potential: float32 [32768], P('dom'), may hold values from 0.5 to 3
- cell_nodes: int32 [128, 512], P('dom'), may hold values from 0 to 5119, as said below
- face_nodes: int32 [32, 256], P('dom'), may hold values from -1 to 4095, as said below
Outputs:
- rotated: float32 [65536, 256], P(('kpt', 'dom'), 'band'), parts along dimension 0
The draws below stay inside these ranges and needn't reach their ends.
There are 2 independent parts, one for each index of `kpt`. The reference program is written for one: setup_inputs(seed, part) draws one part's arguments, and reference() takes and returns one part's arrays. A program takes and returns all parts, laid end to end along the dimension named above; an argument that names none is the same for every part. Nothing has to cross between parts.
Inputs may be any that keep to these rules, and one draw needn't show every extreme that they name: `face_nodes`: row 4 d + o lists in its first slots the own nodes (0 to 4095 of block d) sent to block d + (1, -1, 2, -2)[o]; the remaining slots hold -1; at least one row whose neighbour block exists is full. `cell_nodes`: entries below 4096 are own nodes of the cell's block, the others ghost rows of its extended block. bounds[1] exceeds bounds[0] by 8 or more. `cell_matrix`: symmetric.
All inputs are finite; a program needn't handle non-finite values.
Results may differ from the reference program's by a relative error of at most 0.0054.
Values may be sent and summed in bfloat16 or wider, within the bound.
A program may use at most 64 MiB of HBM per device.

```python
import math
import jax
import jax.numpy as jnp
from jax import lax

NC = 512
BANDS = 256
NODE_DEV = 4096
CELLS = 16
SLOT = 256
NODES = 32768
CELLS_ALL = 128
FACE_ROWS = 32


def draw_wavefunctions(key, part):
    key_one, key_two, key_three = jax.random.split(jax.random.fold_in(key, 5), 3)
    col_scale = jnp.exp(jax.random.uniform(key_two, (BANDS,), jnp.float32, math.log(0.3), math.log(3.0)))
    row_scale = jnp.exp(jax.random.uniform(key_three, (NODES,), jnp.float32, math.log(0.3), math.log(3.0)))
    values = jax.random.truncated_normal(key_one, -4.0, 4.0, (NODES, BANDS), jnp.float32)
    return (values * row_scale[:, None] * col_scale[None, :]).astype(jnp.bfloat16)


def draw_bounds(key, part):
    draws = jax.random.uniform(jax.random.fold_in(key, 21), (2,), jnp.float32)
    low_end = 0.5 + 2.5 * draws[0]
    high_end = low_end + 8.0 + 12.0 * draws[1]
    return jnp.stack([low_end, high_end]).astype(jnp.float32)


def draw_cell_matrix(key, part):
    inner = jax.random.fold_in(key, 31)
    values = jax.random.truncated_normal(inner, -4.0, 4.0, (NC, NC), jnp.float32)
    matrix = (values + values.T) / math.sqrt(2.0 * NC) + 2.5 * jnp.eye(NC, dtype=jnp.float32)
    return matrix.astype(jnp.bfloat16)


def draw_cell_scale(key, part):
    inner = jax.random.fold_in(key, 41)
    position = jnp.arange(CELLS_ALL).astype(jnp.float32)
    rising = jnp.exp(math.log(3.0) * position / max(CELLS_ALL - 1, 1))
    factor = jnp.exp(jax.random.uniform(inner, (CELLS_ALL,), jnp.float32, math.log(0.5), math.log(2.0)))
    return (rising * factor).astype(jnp.float32)


def draw_cell_nodes(key, part):
    key_one, key_two, key_three, key_four, key_five = jax.random.split(jax.random.fold_in(key, 51), 5)
    cell_keys = jax.random.split(key_one, CELLS_ALL)
    orders = jax.vmap(lambda single: jax.random.permutation(single, NC))(cell_keys).astype(jnp.int32)
    base = jnp.arange(CELLS_ALL, dtype=jnp.int32) % CELLS * (NC // 2)
    owned = (base[:, None] + orders) % NODE_DEV
    chosen = jax.random.randint(key_two, (CELLS_ALL, NC), 0, 4) == 0
    ghost_rows = NODE_DEV + jax.random.randint(key_three, (CELLS_ALL, NC), 0, 4 * SLOT)
    result = jnp.where(chosen, ghost_rows, owned).astype(jnp.int32).reshape(-1)
    total = CELLS_ALL * NC
    low_spot = jax.random.randint(key_four, (), 0, total // 2)
    high_spot = jax.random.randint(key_five, (), total // 2, total)
    result = result.at[low_spot].set(0)
    result = result.at[high_spot].set(NODE_DEV + 4 * SLOT - 1)
    return result.reshape(CELLS_ALL, NC).astype(jnp.int32)


def draw_face_nodes(key, part):
    key_one, key_two, key_three, key_four = jax.random.split(jax.random.fold_in(key, 61), 4)
    lengths = jax.random.randint(key_one, (FACE_ROWS,), SLOT // 4, SLOT)
    block_pick = jax.random.randint(key_two, (), 2, FACE_ROWS // 4 - 2)
    offset_pick = jax.random.randint(key_three, (), 0, 4)
    full_row = 4 * block_pick + offset_pick
    lengths = jnp.where(jnp.arange(FACE_ROWS, dtype=jnp.int32) == full_row, SLOT, lengths)
    entries = jax.random.randint(key_four, (FACE_ROWS, SLOT), 0, NODE_DEV)
    entries = entries.at[full_row, 0].set(NODE_DEV - 1)
    slot_ids = jnp.arange(SLOT, dtype=jnp.int32)[None, :]
    return jnp.where(slot_ids < lengths[:, None], entries, -1).astype(jnp.int32)


def block_scale(key, shape, cuts, low, top_value):
    def one(axis_at, parts):
        steps = jax.random.uniform(jax.random.fold_in(jax.random.fold_in(key, 6), axis_at), (parts,), jnp.float32, low / len(cuts), top_value / len(cuts))
        return jnp.repeat(jnp.exp(steps), shape[axis_at] // parts).reshape((-1,) + (1,) * (len(shape) - axis_at - 1))

    gain = one(*cuts[0])
    for cut in cuts[1:]:
        gain = gain * one(*cut)
    return gain


def setup_inputs(seed: int = 0, part: int = 0) -> dict:
    seeds = jax.random.split(jax.random.key(seed), 8)
    own_keys = jax.random.split(jax.random.fold_in(seeds[7], part), 8)
    return {
        "wavefunctions": draw_wavefunctions(jax.random.fold_in(jax.random.fold_in(seeds[7], part), 71), part),
        "bounds": draw_bounds(jax.random.fold_in(jax.random.fold_in(seeds[7], part), 71), part),
        "cell_matrix": draw_cell_matrix(jax.random.fold_in(seeds[7], 71), part),
        "cell_scale": draw_cell_scale(jax.random.fold_in(seeds[7], 71), part),
        "potential": jnp.clip(0.5 + 2.5 * jax.random.uniform(seeds[4], (NODES,), jnp.float32) ** block_scale(seeds[4], (NODES,), ((0, 8),), -0.2, 0.2), 0.5, 3.0),
        "cell_nodes": draw_cell_nodes(jax.random.fold_in(seeds[7], 71), part),
        "face_nodes": draw_face_nodes(jax.random.fold_in(seeds[7], 71), part),
    }


peer_offsets = (1, -1, 2, -2)

def shift_devices(blocks, offset):
    padding = jnp.zeros_like(blocks[:abs(offset)])
    if offset > 0:
        return jnp.concatenate([padding, blocks[:-offset]], 0)
    return jnp.concatenate([blocks[-offset:], padding], 0)

def apply_operator(vectors, cell_matrix, cell_scale, potential, cell_nodes, face_nodes):
    node_blocks = NODES // NODE_DEV
    blocks = vectors.reshape(node_blocks, NODE_DEV, BANDS)
    faces = face_nodes.reshape(node_blocks, 4, SLOT)
    filled = faces >= 0
    safe_index = jnp.maximum(faces, 0)
    outgoing = jax.vmap(lambda block_rows, picks: block_rows[picks])(blocks, safe_index)
    outgoing = jnp.where(filled[..., None], outgoing, jnp.zeros((), vectors.dtype))
    ghosts = jnp.stack([shift_devices(outgoing[:, idx], peer_offsets[idx]) for idx in range(4)], 1)
    extended = jnp.concatenate([blocks, ghosts.reshape(node_blocks, 4 * SLOT, BANDS)], 1)
    cell_maps = cell_nodes.reshape(node_blocks, CELLS, NC)
    scales = cell_scale.reshape(node_blocks, CELLS)
    stiffness = cell_matrix.astype(jnp.float32)

    def cell_pass(device_items):
        ext_rows, maps, scale_row = device_items
        gathered = ext_rows[maps].astype(jnp.float32)
        products = jnp.einsum('ij,cjk->cik', stiffness, gathered) * scale_row[:, None, None]
        return jax.ops.segment_sum(products.reshape(-1, BANDS), maps.reshape(-1), num_segments=NODE_DEV + 4 * SLOT)
    summed = lax.map(cell_pass, (extended, cell_maps, scales))
    owned = summed[:, :NODE_DEV]
    ghost_acc = summed[:, NODE_DEV:].reshape(node_blocks, 4, SLOT, BANDS)
    returned = jnp.stack([shift_devices(ghost_acc[:, idx], -peer_offsets[idx]) for idx in range(4)], 1)
    targets = jnp.where(filled, faces, NODE_DEV).astype(jnp.int32)

    def add_back(owned_rows, returned_rows, target_rows):
        extra = jax.ops.segment_sum(returned_rows.reshape(-1, BANDS), target_rows.reshape(-1), num_segments=NODE_DEV + 1)
        return owned_rows + extra[:NODE_DEV]
    owned = jax.vmap(add_back)(owned, returned, targets)
    return owned.reshape(NODES, BANDS) + potential[:, None] * vectors.astype(jnp.float32)

def reference(wavefunctions, bounds, cell_matrix, cell_scale, potential, cell_nodes, face_nodes):
    center = (bounds[0] + bounds[1]) / 2.0
    half_width = (bounds[1] - bounds[0]) / 2.0
    wave_wide = wavefunctions.astype(jnp.float32)
    image_one = apply_operator(wavefunctions, cell_matrix, cell_scale, potential, cell_nodes, face_nodes)
    degree_one = ((image_one - center * wave_wide) / half_width).astype(jnp.bfloat16)
    image_two = apply_operator(degree_one, cell_matrix, cell_scale, potential, cell_nodes, face_nodes)
    degree_two = (2.0 * (image_two - center * degree_one.astype(jnp.float32)) / half_width - wave_wide).astype(jnp.bfloat16)
    margin = jnp.dot(degree_two.T.astype(jnp.float32), degree_two.astype(jnp.float32), preferred_element_type=jnp.float32) / NODES
    factor = jnp.linalg.cholesky(margin)
    inverse = lax.linalg.triangular_solve(factor, jnp.eye(BANDS, dtype=factor.dtype), left_side=True, lower=True)
    return jnp.dot(degree_two.astype(jnp.float32), inverse.T, precision=lax.Precision.HIGHEST)
```

```python
import functools

import jax
import jax.numpy as jnp
from jax import lax
from jax.experimental import pallas as pl
from jax.experimental.pallas import tpu as pltpu
from jax.sharding import PartitionSpec as P

peer_offsets = (1, -1, 2, -2)
MESH = pl.DeviceIdType.MESH
VM = pl.BlockSpec(memory_space=pltpu.VMEM)
SM = pl.BlockSpec(memory_space=pltpu.SMEM)
ACCS = 8


def params(**more):
    return pltpu.CompilerParams(vmem_limit_bytes=50 * 1024 * 1024, **more)


def chunks(total, size, body):
    def step(i, carry):
        body(pl.ds(pl.multiple_of(i * size, size), size))
        return carry

    lax.fori_loop(0, total // size, step, 0)


def exchange_kernel(sign, send_ref, recv_ref, send_sem, recv_sem):
    me = lax.axis_index("dom")
    size = lax.axis_size("dom")
    slot = send_ref.shape[0] // 4
    barrier = pltpu.get_barrier_semaphore()

    def exists(by):
        there = me + by
        return jnp.logical_and(there >= 0, there < size)

    for by in peer_offsets:

        @pl.when(exists(by))
        def _():
            pl.semaphore_signal(
                barrier, inc=1, device_id={"dom": me + by}, device_id_type=MESH
            )

    peers = jnp.int32(0)
    for by in peer_offsets:
        peers = peers + exists(by).astype(jnp.int32)
    pl.semaphore_wait(barrier, peers)

    def copy(o, by):
        rows = pl.ds(o * slot, slot)
        return pltpu.make_async_remote_copy(
            src_ref=send_ref.at[rows],
            dst_ref=recv_ref.at[rows],
            send_sem=send_sem.at[o],
            recv_sem=recv_sem.at[o],
            device_id={"dom": me + by},
            device_id_type=MESH,
        )

    for o in (2, 3, 0, 1):
        by = sign * peer_offsets[o]

        @pl.when(exists(by))
        def _():
            copy(o, by).start()

    for o in range(4):
        by = sign * peer_offsets[o]

        @pl.when(jnp.logical_not(exists(-by)))
        def _():
            recv_ref[pl.ds(o * slot, slot), :] = jnp.zeros(
                (slot, recv_ref.shape[1]), recv_ref.dtype
            )

    for o in range(4):
        by = sign * peer_offsets[o]

        @pl.when(exists(by))
        def _():
            copy(o, by).wait_send()

        @pl.when(exists(-by))
        def _():
            copy(o, by).wait_recv()


def exchange(values, sign):
    return pl.pallas_call(
        functools.partial(exchange_kernel, sign),
        out_shape=jax.ShapeDtypeStruct(values.shape, values.dtype),
        in_specs=[VM],
        out_specs=VM,
        scratch_shapes=[pltpu.SemaphoreType.DMA((4,)), pltpu.SemaphoreType.DMA((4,))],
        compiler_params=params(collective_id=1 if sign > 0 else 2, has_side_effects=True),
        name="exchange_out" if sign > 0 else "exchange_back",
    )(values)


def gather_faces(wide, targets_ref, stage, out_ref):
    group = 16

    def step(i, carry):
        base = pl.multiple_of(i * group, group)
        rows = [wide[pl.ds(targets_ref[base + u], 1), :] for u in range(group)]
        for u in range(group):
            stage[pl.ds(base + u, 1), :] = rows[u]
        return carry

    lax.fori_loop(0, stage.shape[0] // group, step, 0)

    def cast(rows):
        out_ref[rows, :] = stage[rows, :].astype(out_ref.dtype)

    chunks(stage.shape[0], 128, cast)


def faces_kernel(v_ref, targets_ref, out_ref, wide, stage):
    nodes = v_ref.shape[0]

    def widen(rows):
        wide[rows, :] = v_ref[rows, :].astype(jnp.float32)

    chunks(nodes, 256, widen)
    wide[pl.ds(nodes, 8), :] = jnp.zeros((8, wide.shape[1]), jnp.float32)
    gather_faces(wide, targets_ref, stage, out_ref)


def faces_of(v, targets):
    nodes, columns = v.shape
    count = targets.shape[0]
    return pl.pallas_call(
        faces_kernel,
        out_shape=jax.ShapeDtypeStruct((count, columns), v.dtype),
        in_specs=[VM, SM],
        out_specs=VM,
        scratch_shapes=[
            pltpu.VMEM((nodes + 8, columns), jnp.float32),
            pltpu.VMEM((count, columns), jnp.float32),
        ],
        compiler_params=params(),
        name="faces",
    )(v, targets)


def operate_kernel(
    v_ref, ghost_ref, matrix_ref, maps_ref, scale_ref, own_ref, back_ref, ext, *rest
):
    nodes, columns = v_ref.shape
    ghosts = ghost_ref.shape[0]
    nc = matrix_ref.shape[0]
    cells = scale_ref.shape[0]
    group = 8
    gat, prod, accs = rest[:2], rest[2:4], rest[4:]

    def widen(rows):
        ext[rows, :] = v_ref[rows, :].astype(jnp.float32)

    chunks(nodes, 256, widen)
    for part in range(ghosts // 256):
        ext[pl.ds(nodes + part * 256, 256), :] = ghost_ref[pl.ds(part * 256, 256), :].astype(
            jnp.float32
        )

    def clear(rows):
        for acc in accs:
            acc[rows, :] = jnp.zeros((64, columns), jnp.float32)

    chunks(nodes + ghosts, 64, clear)

    def gather_step(pair, base):
        rows = [
            (u, h, ext[pl.ds(maps_ref[(2 * pair + h) * nc + base + u], 1), :])
            for u in range(group)
            for h in range(2)
        ]
        for u, h, row in rows:
            gat[h][pl.ds(base + u, 1), :] = row

    def scatter_step(pair, base):
        for first in range(0, group, ACCS // 2):
            spots = []
            for u in range(ACCS // 2):
                for h in range(2):
                    at = pl.ds(maps_ref[(2 * pair + h) * nc + base + first + u], 1)
                    acc = accs[2 * u + h]
                    spots.append(
                        (acc, at, acc[at, :] + prod[h][pl.ds(base + first + u, 1), :])
                    )
            for acc, at, value in spots:
                acc[at, :] = value

    def rows_loop(body):
        def step(i, carry):
            body(pl.multiple_of(i * group, group))
            return carry

        lax.fori_loop(0, nc // group, step, 0)

    def multiply(pair):
        both = jnp.concatenate([gat[0][...], gat[1][...]], 1).astype(jnp.bfloat16)
        result = jnp.dot(matrix_ref[...], both, preferred_element_type=jnp.float32)
        for h in range(2):
            prod[h][...] = (
                result[:, h * columns : (h + 1) * columns] * scale_ref[2 * pair + h]
            )

    rows_loop(lambda base: gather_step(0, base))

    def pair_step(pair, carry):
        multiply(pair)

        def both(base):
            gather_step(pair + 1, base)
            scatter_step(pair, base)

        rows_loop(both)
        return carry

    last = cells // 2 - 1
    lax.fori_loop(0, last, pair_step, 0)
    multiply(last)
    rows_loop(lambda base: scatter_step(last, base))

    def total(rows):
        value = accs[0][rows, :]
        for acc in accs[1:]:
            value = value + acc[rows, :]
        return value

    def collect(rows):
        own_ref[rows, :] = total(rows)

    chunks(nodes, 64, collect)
    for part in range(ghosts // 64):
        back_ref[pl.ds(part * 64, 64), :] = total(pl.ds(nodes + part * 64, 64))


def operate(v, ghosts, matrix, maps, scale):
    nodes, columns = v.shape
    count = ghosts.shape[0]
    nc = matrix.shape[0]
    return pl.pallas_call(
        operate_kernel,
        out_shape=(
            jax.ShapeDtypeStruct((nodes, columns), jnp.float32),
            jax.ShapeDtypeStruct((count, columns), jnp.float32),
        ),
        in_specs=[VM, VM, VM, SM, SM],
        out_specs=(VM, VM),
        scratch_shapes=[
            pltpu.VMEM((nodes + count, columns), jnp.float32),
        ]
        + [pltpu.VMEM((nc, columns), jnp.float32)] * 4
        + [pltpu.VMEM((nodes + count, columns), jnp.float32)] * ACCS,
        compiler_params=params(),
        name="operate",
    )(v, ghosts, matrix, maps, scale)


def combine_kernel(first, own_ref, back_ref, v_ref, w_ref, diag_ref, targets_ref, coef_ref, *rest):
    nodes, columns = v_ref.shape
    count = back_ref.shape[0]
    slot = count // 4
    if first:
        out_ref, faces_ref, wide, stage = rest[:4]
    else:
        out_ref = rest[0]
    accs = rest[-4:]
    group = 4

    def fill(rows):
        accs[0][rows, :] = own_ref[rows, :]
        for acc in accs[1:]:
            acc[rows, :] = jnp.zeros((64, columns), jnp.float32)

    chunks(nodes, 64, fill)

    def step(i, carry):
        for u in range(group):
            spots = []
            for o in range(4):
                row = i * group + u + o * slot
                at = pl.ds(targets_ref[row], 1)
                spots.append((accs[o], at, accs[o][at, :] + back_ref[pl.ds(row, 1), :]))
            for acc, at, value in spots:
                acc[at, :] = value
        return carry

    lax.fori_loop(0, slot // group, step, 0)
    coef = coef_ref[0]

    def finish(rows):
        total = (accs[0][rows, :] + accs[1][rows, :]) + (accs[2][rows, :] + accs[3][rows, :])
        image = total * coef + diag_ref[rows, :] * v_ref[rows, :].astype(jnp.float32)
        if first:
            value = image.astype(jnp.bfloat16)
            wide[rows, :] = value.astype(jnp.float32)
        else:
            value = (2.0 * image - w_ref[rows, :].astype(jnp.float32)).astype(jnp.bfloat16)
        out_ref[rows, :] = value

    chunks(nodes, 64, finish)
    if first:
        wide[pl.ds(nodes, 8), :] = jnp.zeros((8, columns), jnp.float32)
        gather_faces(wide, targets_ref, stage, faces_ref)


def combine(first, own, back, v, w, diag, targets, coef):
    nodes, columns = v.shape
    count = back.shape[0]
    value = jax.ShapeDtypeStruct((nodes, columns), jnp.bfloat16)
    faces = jax.ShapeDtypeStruct((count, columns), jnp.bfloat16)
    extra = [
        pltpu.VMEM((nodes + 8, columns), jnp.float32),
        pltpu.VMEM((count, columns), jnp.float32),
    ]
    return pl.pallas_call(
        functools.partial(combine_kernel, first),
        out_shape=(value, faces) if first else value,
        in_specs=[VM, VM, VM, VM, VM, SM, SM],
        out_specs=(VM, VM) if first else VM,
        scratch_shapes=(extra if first else [])
        + [pltpu.VMEM((nodes + 8, columns), jnp.float32)] * 4,
        compiler_params=params(),
        name="combine_one" if first else "combine_two",
    )(own, back, v, w, diag, targets, coef)


def margin_kernel(scaling, x_ref, other_ref, margin_ref, part, slots, send_sem, recv_sem):
    columns = x_ref.shape[1]
    nodes = x_ref.shape[0]
    half_rows = columns // 2
    me = lax.axis_index("dom")
    mine = lax.axis_index("band")
    size = lax.axis_size("dom")
    bits = size.bit_length() - 1
    partners = [{"band": 1 - mine}]
    for k in range(bits):
        bit = 1 << k
        partners.append({"dom": me + bit - 2 * bit * (lax.div(me, bit) % 2)})

    barrier = pltpu.get_barrier_semaphore()
    for partner in partners:
        pl.semaphore_signal(barrier, inc=1, device_id=partner, device_id_type=MESH)
    pl.semaphore_wait(barrier, len(partners))

    def send(at, src, dst, partner):
        copy = pltpu.make_async_remote_copy(
            src_ref=src,
            dst_ref=dst,
            send_sem=send_sem.at[at],
            recv_sem=recv_sem.at[at],
            device_id=partner,
            device_id_type=MESH,
        )
        copy.start()
        return copy

    panel = send(0, x_ref, other_ref, partners[0])
    size_k = 512

    def product(right, lanes):
        def step(i, total):
            rows = pl.ds(pl.multiple_of(i * size_k, size_k), size_k)
            return total + lax.dot_general(
                x_ref[rows, :],
                right[rows, :],
                (((0,), (0,)), ((), ())),
                preferred_element_type=jnp.float32,
            )

        part[:, lanes] = lax.fori_loop(
            0, nodes // size_k, step, jnp.zeros((columns, columns), jnp.float32)
        )

    product(x_ref, pl.ds(0, columns))
    panel.wait()
    product(other_ref, pl.ds(columns, columns))

    low = me % 2
    keep = pl.ds(pl.multiple_of(low * half_rows, half_rows), half_rows)
    give = pl.ds(pl.multiple_of((1 - low) * half_rows, half_rows), half_rows)
    copy = send(1, part.at[give], slots.at[0], partners[1])
    copy.wait()
    part[keep, :] += slots[0]
    for k in range(1, bits):
        copy = send(1 + k, part.at[keep], slots.at[k], partners[1 + k])
        copy.wait()
        part[keep, :] += slots[k]
    copy = send(1 + bits, part.at[keep], slots.at[bits], partners[1])
    copy.wait()
    part[give, :] = slots[bits]
    part[...] = part[...] * scaling
    rows_mine = pl.ds(pl.multiple_of(mine * columns, columns), columns)
    rows_other = pl.ds(pl.multiple_of((1 - mine) * columns, columns), columns)
    copy = send(2 + bits, part, margin_ref.at[rows_mine], partners[0])
    margin_ref[rows_mine, :] = part[...]
    copy.wait()


def margin_of(x, scaling):
    nodes, columns = x.shape
    size = lax.axis_size("dom")
    bits = size.bit_length() - 1
    return pl.pallas_call(
        functools.partial(margin_kernel, scaling),
        out_shape=(
            jax.ShapeDtypeStruct((nodes, columns), x.dtype),
            jax.ShapeDtypeStruct((2 * columns, 2 * columns), jnp.float32),
        ),
        in_specs=[VM],
        out_specs=(VM, VM),
        scratch_shapes=[
            pltpu.VMEM((columns, 2 * columns), jnp.float32),
            pltpu.VMEM((bits + 1, columns // 2, 2 * columns), jnp.float32),
            pltpu.SemaphoreType.DMA((bits + 3,)),
            pltpu.SemaphoreType.DMA((bits + 3,)),
        ],
        compiler_params=params(collective_id=3, has_side_effects=True),
        name="margin",
    )(x)


def on_device(wavefunctions, bounds, cell_matrix, cell_scale, potential, cell_nodes, face_nodes):
    nodes, columns = wavefunctions.shape
    targets = jnp.where(face_nodes >= 0, face_nodes, nodes).reshape(-1)
    maps = cell_nodes.reshape(-1)
    center = (bounds[0] + bounds[1]) / 2.0
    coef = 1.0 / ((bounds[1] - bounds[0]) / 2.0)
    diag = jnp.broadcast_to(((potential - center) * coef)[:, None], (nodes, columns))
    coef = coef.reshape(1)

    def apply_sums(vectors, faces):
        ghosts = exchange(faces, 1)
        own, back = operate(vectors, ghosts, cell_matrix, maps, cell_scale)
        return own, exchange(back, -1)

    own, back = apply_sums(wavefunctions, faces_of(wavefunctions, targets))
    one, faces = combine(True, own, back, wavefunctions, wavefunctions, diag, targets, coef)
    own, back = apply_sums(one, faces)
    two = combine(False, own, back, one, wavefunctions, diag, targets, coef)
    other, margin = margin_of(two, 1.0 / (nodes * lax.axis_size("dom")))
    mine = lax.axis_index("band")
    left, right = margin[:columns], margin[columns:]
    right = jnp.concatenate([right[:, columns:], right[:, :columns]], 1)
    margin = jnp.concatenate([left, right], 0)
    factor = jnp.linalg.cholesky(margin)
    band_count = margin.shape[0]
    inverse = lax.linalg.triangular_solve(
        factor, jnp.eye(band_count, dtype=factor.dtype), left_side=True, lower=True
    )
    own_rows = lax.dynamic_slice_in_dim(inverse, mine * columns, columns, 0)
    own_part = lax.dynamic_slice_in_dim(own_rows, mine * columns, columns, 1)
    other_part = lax.dynamic_slice_in_dim(own_rows, (1 - mine) * columns, columns, 1)
    panel = jnp.concatenate([two, other], 1)
    rows = jnp.concatenate([own_part, other_part], 1)
    high = rows.astype(jnp.bfloat16)
    low = (rows - high.astype(jnp.float32)).astype(jnp.bfloat16)
    return jnp.dot(panel, high.T, preferred_element_type=jnp.float32) + jnp.dot(
        panel, low.T, preferred_element_type=jnp.float32
    )


def solution(mesh):
    return jax.shard_map(
        on_device,
        mesh=mesh,
        in_specs=(
            P(("kpt", "dom"), "band"),
            P("kpt"),
            P(),
            P("dom"),
            P("dom"),
            P("dom", None),
            P("dom", None),
        ),
        out_specs=P(("kpt", "dom"), "band"),
        check_vma=False,
    )
```

```python
import functools

import jax
import jax.numpy as jnp
from jax import lax
from jax.experimental import pallas as pl
from jax.experimental.pallas import tpu as pltpu
from jax.sharding import PartitionSpec as P

peer_offsets = (1, -1, 2, -2)
MESH = pl.DeviceIdType.MESH
VM = pl.BlockSpec(memory_space=pltpu.VMEM)
SM = pl.BlockSpec(memory_space=pltpu.SMEM)
ACCS = 8


def params(**more):
    return pltpu.CompilerParams(vmem_limit_bytes=50 * 1024 * 1024, **more)


def chunks(total, size, body):
    def step(i, carry):
        body(pl.ds(pl.multiple_of(i * size, size), size))
        return carry

    lax.fori_loop(0, total // size, step, 0)


def exchange_kernel(sign, send_ref, recv_ref, send_sem, recv_sem):
    me = lax.axis_index("dom")
    size = lax.axis_size("dom")
    slot = send_ref.shape[0] // 4
    barrier = pltpu.get_barrier_semaphore()

    def exists(by):
        there = me + by
        return jnp.logical_and(there >= 0, there < size)

    for by in peer_offsets:

        @pl.when(exists(by))
        def _():
            pl.semaphore_signal(
                barrier, inc=1, device_id={"dom": me + by}, device_id_type=MESH
            )

    peers = jnp.int32(0)
    for by in peer_offsets:
        peers = peers + exists(by).astype(jnp.int32)
    pl.semaphore_wait(barrier, peers)

    def copy(o, by):
        rows = pl.ds(o * slot, slot)
        return pltpu.make_async_remote_copy(
            src_ref=send_ref.at[rows],
            dst_ref=recv_ref.at[rows],
            send_sem=send_sem.at[o],
            recv_sem=recv_sem.at[o],
            device_id={"dom": me + by},
            device_id_type=MESH,
        )

    for o in (2, 3, 0, 1):
        by = sign * peer_offsets[o]

        @pl.when(exists(by))
        def _():
            copy(o, by).start()

    for o in range(4):
        by = sign * peer_offsets[o]

        @pl.when(jnp.logical_not(exists(-by)))
        def _():
            recv_ref[pl.ds(o * slot, slot), :] = jnp.zeros(
                (slot, recv_ref.shape[1]), recv_ref.dtype
            )

    for o in range(4):
        by = sign * peer_offsets[o]

        @pl.when(exists(by))
        def _():
            copy(o, by).wait_send()

        @pl.when(exists(-by))
        def _():
            copy(o, by).wait_recv()


def exchange(values, sign):
    return pl.pallas_call(
        functools.partial(exchange_kernel, sign),
        out_shape=jax.ShapeDtypeStruct(values.shape, values.dtype),
        in_specs=[VM],
        out_specs=VM,
        scratch_shapes=[pltpu.SemaphoreType.DMA((4,)), pltpu.SemaphoreType.DMA((4,))],
        compiler_params=params(collective_id=1 if sign > 0 else 2, has_side_effects=True),
        name="exchange_out" if sign > 0 else "exchange_back",
    )(values)


def gather_faces(wide, targets_ref, stage, out_ref):
    group = 16

    def step(i, carry):
        base = pl.multiple_of(i * group, group)
        rows = [wide[pl.ds(targets_ref[base + u], 1), :] for u in range(group)]
        for u in range(group):
            stage[pl.ds(base + u, 1), :] = rows[u]
        return carry

    lax.fori_loop(0, stage.shape[0] // group, step, 0)

    def cast(rows):
        out_ref[rows, :] = stage[rows, :].astype(out_ref.dtype)

    chunks(stage.shape[0], 128, cast)


def faces_kernel(v_ref, targets_ref, out_ref, wide, stage):
    nodes = v_ref.shape[0]

    def widen(rows):
        wide[rows, :] = v_ref[rows, :].astype(jnp.float32)

    chunks(nodes, 256, widen)
    wide[pl.ds(nodes, 8), :] = jnp.zeros((8, wide.shape[1]), jnp.float32)
    gather_faces(wide, targets_ref, stage, out_ref)


def faces_of(v, targets):
    nodes, columns = v.shape
    count = targets.shape[0]
    return pl.pallas_call(
        faces_kernel,
        out_shape=jax.ShapeDtypeStruct((count, columns), v.dtype),
        in_specs=[VM, SM],
        out_specs=VM,
        scratch_shapes=[
            pltpu.VMEM((nodes + 8, columns), jnp.float32),
            pltpu.VMEM((count, columns), jnp.float32),
        ],
        compiler_params=params(),
        name="faces",
    )(v, targets)


def operate_kernel(
    v_ref, ghost_ref, matrix_ref, maps_ref, scale_ref, own_ref, back_ref, ext, *rest
):
    nodes, columns = v_ref.shape
    ghosts = ghost_ref.shape[0]
    nc = matrix_ref.shape[0]
    cells = scale_ref.shape[0]
    group = 8
    gat, prod, accs = rest[:2], rest[2:4], rest[4:]

    def widen(rows):
        ext[rows, :] = v_ref[rows, :].astype(jnp.float32)

    chunks(nodes, 256, widen)
    for part in range(ghosts // 256):
        ext[pl.ds(nodes + part * 256, 256), :] = ghost_ref[pl.ds(part * 256, 256), :].astype(
            jnp.float32
        )

    def clear(rows):
        for acc in accs:
            acc[rows, :] = jnp.zeros((64, columns), jnp.float32)

    chunks(nodes + ghosts, 64, clear)

    def gather_step(pair, base):
        rows = [
            (u, h, ext[pl.ds(maps_ref[(2 * pair + h) * nc + base + u], 1), :])
            for u in range(group)
            for h in range(2)
        ]
        for u, h, row in rows:
            gat[h][pl.ds(base + u, 1), :] = row

    def scatter_step(pair, base):
        for first in range(0, group, ACCS // 2):
            spots = []
            for u in range(ACCS // 2):
                for h in range(2):
                    at = pl.ds(maps_ref[(2 * pair + h) * nc + base + first + u], 1)
                    acc = accs[2 * u + h]
                    spots.append(
                        (acc, at, acc[at, :] + prod[h][pl.ds(base + first + u, 1), :])
                    )
            for acc, at, value in spots:
                acc[at, :] = value

    def rows_loop(body):
        def step(i, carry):
            body(pl.multiple_of(i * group, group))
            return carry

        lax.fori_loop(0, nc // group, step, 0)

    def multiply(pair):
        both = jnp.concatenate([gat[0][...], gat[1][...]], 1).astype(jnp.bfloat16)
        result = jnp.dot(matrix_ref[...], both, preferred_element_type=jnp.float32)
        for h in range(2):
            prod[h][...] = (
                result[:, h * columns : (h + 1) * columns] * scale_ref[2 * pair + h]
            )

    rows_loop(lambda base: gather_step(0, base))

    def pair_step(pair, carry):
        multiply(pair)

        def both(base):
            gather_step(pair + 1, base)
            scatter_step(pair, base)

        rows_loop(both)
        return carry

    last = cells // 2 - 1
    lax.fori_loop(0, last, pair_step, 0)
    multiply(last)
    rows_loop(lambda base: scatter_step(last, base))

    def total(rows):
        value = accs[0][rows, :]
        for acc in accs[1:]:
            value = value + acc[rows, :]
        return value

    def collect(rows):
        own_ref[rows, :] = total(rows)

    chunks(nodes, 64, collect)
    for part in range(ghosts // 64):
        back_ref[pl.ds(part * 64, 64), :] = total(pl.ds(nodes + part * 64, 64))


def operate(v, ghosts, matrix, maps, scale):
    nodes, columns = v.shape
    count = ghosts.shape[0]
    nc = matrix.shape[0]
    return pl.pallas_call(
        operate_kernel,
        out_shape=(
            jax.ShapeDtypeStruct((nodes, columns), jnp.float32),
            jax.ShapeDtypeStruct((count, columns), jnp.float32),
        ),
        in_specs=[VM, VM, VM, SM, SM],
        out_specs=(VM, VM),
        scratch_shapes=[
            pltpu.VMEM((nodes + count, columns), jnp.float32),
        ]
        + [pltpu.VMEM((nc, columns), jnp.float32)] * 4
        + [pltpu.VMEM((nodes + count, columns), jnp.float32)] * ACCS,
        compiler_params=params(),
        name="operate",
    )(v, ghosts, matrix, maps, scale)


def combine_kernel(first, own_ref, back_ref, v_ref, w_ref, diag_ref, targets_ref, coef_ref, *rest):
    nodes, columns = v_ref.shape
    count = back_ref.shape[0]
    slot = count // 4
    if first:
        out_ref, faces_ref, wide, stage = rest[:4]
    else:
        out_ref = rest[0]
    accs = rest[-4:]
    group = 4

    def fill(rows):
        accs[0][rows, :] = own_ref[rows, :]
        for acc in accs[1:]:
            acc[rows, :] = jnp.zeros((64, columns), jnp.float32)

    chunks(nodes, 64, fill)

    def step(i, carry):
        for u in range(group):
            spots = []
            for o in range(4):
                row = i * group + u + o * slot
                at = pl.ds(targets_ref[row], 1)
                spots.append((accs[o], at, accs[o][at, :] + back_ref[pl.ds(row, 1), :]))
            for acc, at, value in spots:
                acc[at, :] = value
        return carry

    lax.fori_loop(0, slot // group, step, 0)
    coef = coef_ref[0]

    def finish(rows):
        total = (accs[0][rows, :] + accs[1][rows, :]) + (accs[2][rows, :] + accs[3][rows, :])
        image = total * coef + diag_ref[rows, :] * v_ref[rows, :].astype(jnp.float32)
        if first:
            value = image.astype(jnp.bfloat16)
            wide[rows, :] = value.astype(jnp.float32)
        else:
            value = (2.0 * image - w_ref[rows, :].astype(jnp.float32)).astype(jnp.bfloat16)
        out_ref[rows, :] = value

    chunks(nodes, 64, finish)
    if first:
        wide[pl.ds(nodes, 8), :] = jnp.zeros((8, columns), jnp.float32)
        gather_faces(wide, targets_ref, stage, faces_ref)


def combine(first, own, back, v, w, diag, targets, coef):
    nodes, columns = v.shape
    count = back.shape[0]
    value = jax.ShapeDtypeStruct((nodes, columns), jnp.bfloat16)
    faces = jax.ShapeDtypeStruct((count, columns), jnp.bfloat16)
    extra = [
        pltpu.VMEM((nodes + 8, columns), jnp.float32),
        pltpu.VMEM((count, columns), jnp.float32),
    ]
    return pl.pallas_call(
        functools.partial(combine_kernel, first),
        out_shape=(value, faces) if first else value,
        in_specs=[VM, VM, VM, VM, VM, SM, SM],
        out_specs=(VM, VM) if first else VM,
        scratch_shapes=(extra if first else [])
        + [pltpu.VMEM((nodes + 8, columns), jnp.float32)] * 4,
        compiler_params=params(),
        name="combine_one" if first else "combine_two",
    )(own, back, v, w, diag, targets, coef)


def margin_kernel(scaling, x_ref, other_ref, margin_ref, part, slots, send_sem, recv_sem):
    columns = x_ref.shape[1]
    nodes = x_ref.shape[0]
    half_rows = columns // 2
    me = lax.axis_index("dom")
    mine = lax.axis_index("band")
    size = lax.axis_size("dom")
    bits = size.bit_length() - 1
    partners = [{"band": 1 - mine}]
    for k in range(bits):
        bit = 1 << k
        partners.append({"dom": me + bit - 2 * bit * (lax.div(me, bit) % 2)})

    barrier = pltpu.get_barrier_semaphore()
    for partner in partners:
        pl.semaphore_signal(barrier, inc=1, device_id=partner, device_id_type=MESH)
    pl.semaphore_wait(barrier, len(partners))

    def send(at, src, dst, partner):
        copy = pltpu.make_async_remote_copy(
            src_ref=src,
            dst_ref=dst,
            send_sem=send_sem.at[at],
            recv_sem=recv_sem.at[at],
            device_id=partner,
            device_id_type=MESH,
        )
        copy.start()
        return copy

    panel = send(0, x_ref, other_ref, partners[0])
    size_k = 512

    def product(right, lanes):
        def step(i, total):
            rows = pl.ds(pl.multiple_of(i * size_k, size_k), size_k)
            return total + lax.dot_general(
                x_ref[rows, :],
                right[rows, :],
                (((0,), (0,)), ((), ())),
                preferred_element_type=jnp.float32,
            )

        part[:, lanes] = lax.fori_loop(
            0, nodes // size_k, step, jnp.zeros((columns, columns), jnp.float32)
        )

    product(x_ref, pl.ds(0, columns))
    panel.wait()
    product(other_ref, pl.ds(columns, columns))

    low = me % 2
    keep = pl.ds(pl.multiple_of(low * half_rows, half_rows), half_rows)
    give = pl.ds(pl.multiple_of((1 - low) * half_rows, half_rows), half_rows)
    copy = send(1, part.at[give], slots.at[0], partners[1])
    copy.wait()
    part[keep, :] += slots[0]
    for k in range(1, bits):
        copy = send(1 + k, part.at[keep], slots.at[k], partners[1 + k])
        copy.wait()
        part[keep, :] += slots[k]
    copy = send(1 + bits, part.at[keep], slots.at[bits], partners[1])
    copy.wait()
    part[give, :] = slots[bits]
    rows_mine = pl.ds(pl.multiple_of(mine * columns, columns), columns)
    lanes_other = pl.ds(pl.multiple_of((1 - mine) * columns, columns), columns)
    margin_ref[rows_mine, rows_mine] = part[:, :columns] * scaling
    margin_ref[rows_mine, lanes_other] = part[:, columns:] * scaling
    copy = send(2 + bits, margin_ref.at[rows_mine], margin_ref.at[rows_mine], partners[0])
    copy.wait()


def margin_of(x, scaling):
    nodes, columns = x.shape
    size = lax.axis_size("dom")
    bits = size.bit_length() - 1
    return pl.pallas_call(
        functools.partial(margin_kernel, scaling),
        out_shape=(
            jax.ShapeDtypeStruct((nodes, columns), x.dtype),
            jax.ShapeDtypeStruct((2 * columns, 2 * columns), jnp.float32),
        ),
        in_specs=[VM],
        out_specs=(VM, VM),
        scratch_shapes=[
            pltpu.VMEM((columns, 2 * columns), jnp.float32),
            pltpu.VMEM((bits + 1, columns // 2, 2 * columns), jnp.float32),
            pltpu.SemaphoreType.DMA((bits + 3,)),
            pltpu.SemaphoreType.DMA((bits + 3,)),
        ],
        compiler_params=params(collective_id=3, has_side_effects=True),
        name="margin",
    )(x)


BLOCK = 64


def inverse_factor(block):
    lane = lax.broadcasted_iota(jnp.int32, (8, 2 * BLOCK), 1)
    sub = lax.broadcasted_iota(jnp.int32, (8, 2 * BLOCK), 0)
    doubled = jnp.concatenate([block, block], 1)
    tiles = []
    for t in range(BLOCK // 8):
        unit = (lane - BLOCK == sub + 8 * t).astype(jnp.float32)
        tiles.append(jnp.where(lane < BLOCK, doubled[8 * t : 8 * t + 8], unit))
    for j in range(BLOCK):
        t, u = divmod(j, 8)
        columns = {i: jnp.broadcast_to(tiles[i][:, j : j + 1], (8, 2 * BLOCK)) for i in range(t, BLOCK // 8)}
        pivot = jnp.broadcast_to(columns[t][u : u + 1], (8, 2 * BLOCK))
        row = jnp.broadcast_to(tiles[t][u : u + 1], (8, 2 * BLOCK)) / pivot
        tiles[t] = tiles[t] - jnp.where(sub > u, columns[t], 0.0) * row
        for i in range(t + 1, BLOCK // 8):
            tiles[i] = tiles[i] - columns[i] * row
    scaled = []
    for t, tile in enumerate(tiles):
        diagonal = jnp.sum(jnp.where(lane == sub + 8 * t, tile, 0.0), 1, keepdims=True)
        scaled.append(tile * lax.rsqrt(diagonal))
    return jnp.concatenate(scaled, 0)[:, BLOCK:]


def finish_kernel(margin_ref, x_ref, other_ref, mine_ref, out_ref, work):
    nodes, columns = x_ref.shape
    bands = margin_ref.shape[0]
    exact = lax.Precision.HIGHEST
    work[...] = margin_ref[...]
    for first in range(0, bands, BLOCK):
        last = first + BLOCK
        inverse = inverse_factor(work[first:last, first:last])
        pieces = [inverse]
        if first:
            pieces = [work[first:last, :first]] + pieces
        if last < bands:
            pieces = pieces + [work[first:last, last:]]
        for at, piece in enumerate(pieces):
            if piece is not inverse:
                pieces[at] = jnp.dot(inverse, piece, precision=exact)
        row = jnp.concatenate(pieces, 1) if len(pieces) > 1 else pieces[0]
        lane = lax.broadcasted_iota(jnp.int32, (BLOCK, bands), 1)
        work[first:last, :] = jnp.where(lane < last, row, 0.0)
        if last < bands:
            update = lax.dot_general(
                row[:, last:], row, (((0,), (0,)), ((), ())), precision=exact
            )
            lane = lax.broadcasted_iota(jnp.int32, (bands - last, bands), 1)
            fresh = jnp.logical_and(lane >= first, lane < last)
            work[last:, :] = jnp.where(fresh, 0.0, work[last:, :]) - update

    mine = mine_ref[0]
    own_at = pl.ds(pl.multiple_of(mine * columns, columns), columns)
    other_at = pl.ds(pl.multiple_of((1 - mine) * columns, columns), columns)
    rows = jnp.concatenate([work[own_at, own_at], work[own_at, other_at]], 1)
    high = rows.astype(jnp.bfloat16)
    low = (rows - high.astype(jnp.float32)).astype(jnp.bfloat16)
    both = jnp.concatenate([high, low], 0)

    def rotate(at):
        panel = jnp.concatenate([x_ref[at, :], other_ref[at, :]], 1)
        value = lax.dot_general(
            panel, both, (((1,), (1,)), ((), ())), preferred_element_type=jnp.float32
        )
        out_ref[at, :] = value[:, :columns] + value[:, columns:]

    chunks(nodes, 512, rotate)


def finish(margin, x, other, mine):
    return pl.pallas_call(
        finish_kernel,
        out_shape=jax.ShapeDtypeStruct(x.shape, jnp.float32),
        in_specs=[VM, VM, VM, SM],
        out_specs=VM,
        scratch_shapes=[pltpu.VMEM(margin.shape, jnp.float32)],
        compiler_params=params(),
        name="finish",
    )(margin, x, other, mine)


def on_device(wavefunctions, bounds, cell_matrix, cell_scale, potential, cell_nodes, face_nodes):
    nodes, columns = wavefunctions.shape
    targets = jnp.where(face_nodes >= 0, face_nodes, nodes).reshape(-1)
    maps = cell_nodes.reshape(-1)
    center = (bounds[0] + bounds[1]) / 2.0
    coef = 1.0 / ((bounds[1] - bounds[0]) / 2.0)
    diag = jnp.broadcast_to(((potential - center) * coef)[:, None], (nodes, columns))
    coef = coef.reshape(1)

    def apply_sums(vectors, faces):
        ghosts = exchange(faces, 1)
        own, back = operate(vectors, ghosts, cell_matrix, maps, cell_scale)
        return own, exchange(back, -1)

    own, back = apply_sums(wavefunctions, faces_of(wavefunctions, targets))
    one, faces = combine(True, own, back, wavefunctions, wavefunctions, diag, targets, coef)
    own, back = apply_sums(one, faces)
    two = combine(False, own, back, one, wavefunctions, diag, targets, coef)
    other, margin = margin_of(two, 1.0 / (nodes * lax.axis_size("dom")))
    return finish(margin, two, other, lax.axis_index("band").reshape(1))


def solution(mesh):
    return jax.shard_map(
        on_device,
        mesh=mesh,
        in_specs=(
            P(("kpt", "dom"), "band"),
            P("kpt"),
            P(),
            P("dom"),
            P("dom"),
            P("dom", None),
            P("dom", None),
        ),
        out_specs=P(("kpt", "dom"), "band"),
        check_vma=False,
    )
```

```python
import functools

import jax
import jax.numpy as jnp
from jax import lax
from jax.experimental import pallas as pl
from jax.experimental.pallas import tpu as pltpu
from jax.sharding import PartitionSpec as P

peer_offsets = (1, -1, 2, -2)
MESH = pl.DeviceIdType.MESH
VM = pl.BlockSpec(memory_space=pltpu.VMEM)
SM = pl.BlockSpec(memory_space=pltpu.SMEM)
ACCS = 8


def params(**more):
    return pltpu.CompilerParams(vmem_limit_bytes=50 * 1024 * 1024, **more)


def chunks(total, size, body):
    def step(i, carry):
        body(pl.ds(pl.multiple_of(i * size, size), size))
        return carry

    lax.fori_loop(0, total // size, step, 0)


def exists(by):
    there = lax.axis_index("dom") + by
    return jnp.logical_and(there >= 0, there < lax.axis_size("dom"))


def greet_neighbours(barrier):
    me = lax.axis_index("dom")
    for by in peer_offsets:

        @pl.when(exists(by))
        def _():
            pl.semaphore_signal(
                barrier, inc=1, device_id={"dom": me + by}, device_id_type=MESH
            )


def await_neighbours(barrier):
    peers = jnp.int32(0)
    for by in peer_offsets:
        peers = peers + exists(by).astype(jnp.int32)
    pl.semaphore_wait(barrier, peers)


def face_copy(sign, o, send_ref, recv_ref, send_sem, recv_sem):
    rows = pl.ds(o * (send_ref.shape[0] // 4), send_ref.shape[0] // 4)
    return pltpu.make_async_remote_copy(
        src_ref=send_ref.at[rows],
        dst_ref=recv_ref.at[rows],
        send_sem=send_sem.at[o],
        recv_sem=recv_sem.at[o],
        device_id={"dom": lax.axis_index("dom") + sign * peer_offsets[o]},
        device_id_type=MESH,
    )


def start_face(sign, o, *refs):
    @pl.when(exists(sign * peer_offsets[o]))
    def _():
        face_copy(sign, o, *refs).start()


def end_faces(sign, *refs):
    recv_ref = refs[1]
    slot = recv_ref.shape[0] // 4
    for o in range(4):

        @pl.when(jnp.logical_not(exists(-sign * peer_offsets[o])))
        def _():
            recv_ref[pl.ds(o * slot, slot), :] = jnp.zeros(
                (slot, recv_ref.shape[1]), recv_ref.dtype
            )

    for o in range(4):

        @pl.when(exists(sign * peer_offsets[o]))
        def _():
            face_copy(sign, o, *refs).wait_send()

        @pl.when(exists(-sign * peer_offsets[o]))
        def _():
            face_copy(sign, o, *refs).wait_recv()


def back_kernel(send_ref, recv_ref, send_sem, recv_sem):
    refs = (send_ref, recv_ref, send_sem, recv_sem)
    barrier = pltpu.get_barrier_semaphore()
    greet_neighbours(barrier)
    await_neighbours(barrier)
    for o in (2, 3, 0, 1):
        start_face(-1, o, *refs)
    end_faces(-1, *refs)


def exchange_back(values):
    return pl.pallas_call(
        back_kernel,
        out_shape=jax.ShapeDtypeStruct(values.shape, values.dtype),
        in_specs=[VM],
        out_specs=VM,
        scratch_shapes=[pltpu.SemaphoreType.DMA((4,)), pltpu.SemaphoreType.DMA((4,))],
        compiler_params=params(collective_id=2, has_side_effects=True),
        name="exchange_back",
    )(values)


def out_kernel(v_ref, targets_ref, recv_ref, wide, stage, send, send_sem, recv_sem):
    nodes, columns = v_ref.shape
    slot = send.shape[0] // 4
    group = 16
    refs = (send, recv_ref, send_sem, recv_sem)
    barrier = pltpu.get_barrier_semaphore()
    greet_neighbours(barrier)

    def widen(rows):
        wide[rows, :] = v_ref[rows, :].astype(jnp.float32)

    chunks(nodes, 256, widen)
    wide[pl.ds(nodes, 8), :] = jnp.zeros((8, columns), jnp.float32)
    order = (0, 1, 2, 3)
    for o in order:

        def step(i, carry):
            base = pl.multiple_of(o * slot + i * group, group)
            rows = [wide[pl.ds(targets_ref[base + u], 1), :] for u in range(group)]
            for u in range(group):
                stage[pl.ds(base + u, 1), :] = rows[u]
            return carry

        lax.fori_loop(0, slot // group, step, 0)
        rows = pl.ds(o * slot, slot)
        send[rows, :] = stage[rows, :].astype(send.dtype)
        if o == order[0]:
            await_neighbours(barrier)
        start_face(1, o, *refs)
    end_faces(1, *refs)


def exchange_out(v, targets):
    nodes, columns = v.shape
    count = targets.shape[0]
    return pl.pallas_call(
        out_kernel,
        out_shape=jax.ShapeDtypeStruct((count, columns), v.dtype),
        in_specs=[VM, SM],
        out_specs=VM,
        scratch_shapes=[
            pltpu.VMEM((nodes + 8, columns), jnp.float32),
            pltpu.VMEM((count, columns), jnp.float32),
            pltpu.VMEM((count, columns), v.dtype),
            pltpu.SemaphoreType.DMA((4,)),
            pltpu.SemaphoreType.DMA((4,)),
        ],
        compiler_params=params(collective_id=1, has_side_effects=True),
        name="exchange_out",
    )(v, targets)


def operate_kernel(
    v_ref, ghost_ref, matrix_ref, maps_ref, scale_ref, own_ref, back_ref, ext, *rest
):
    nodes, columns = v_ref.shape
    ghosts = ghost_ref.shape[0]
    nc = matrix_ref.shape[0]
    cells = scale_ref.shape[0]
    group = 8
    gat, prod, accs = rest[:2], rest[2:4], rest[4:]

    def widen(rows):
        ext[rows, :] = v_ref[rows, :].astype(jnp.float32)

    chunks(nodes, 256, widen)
    for part in range(ghosts // 256):
        ext[pl.ds(nodes + part * 256, 256), :] = ghost_ref[pl.ds(part * 256, 256), :].astype(
            jnp.float32
        )

    def clear(rows):
        for acc in accs:
            acc[rows, :] = jnp.zeros((64, columns), jnp.float32)

    chunks(nodes + ghosts, 64, clear)

    def gather_step(pair, base):
        rows = [
            (u, h, ext[pl.ds(maps_ref[(2 * pair + h) * nc + base + u], 1), :])
            for u in range(group)
            for h in range(2)
        ]
        for u, h, row in rows:
            gat[h][pl.ds(base + u, 1), :] = row

    def scatter_step(pair, base):
        for first in range(0, group, ACCS // 2):
            spots = []
            for u in range(ACCS // 2):
                for h in range(2):
                    at = pl.ds(maps_ref[(2 * pair + h) * nc + base + first + u], 1)
                    acc = accs[2 * u + h]
                    spots.append(
                        (acc, at, acc[at, :] + prod[h][pl.ds(base + first + u, 1), :])
                    )
            for acc, at, value in spots:
                acc[at, :] = value

    def rows_loop(body):
        def step(i, carry):
            body(pl.multiple_of(i * group, group))
            return carry

        lax.fori_loop(0, nc // group, step, 0)

    def multiply(pair):
        both = jnp.concatenate([gat[0][...], gat[1][...]], 1).astype(jnp.bfloat16)
        result = jnp.dot(matrix_ref[...], both, preferred_element_type=jnp.float32)
        for h in range(2):
            prod[h][...] = (
                result[:, h * columns : (h + 1) * columns] * scale_ref[2 * pair + h]
            )

    rows_loop(lambda base: gather_step(0, base))

    def pair_step(pair, carry):
        multiply(pair)

        def both(base):
            gather_step(pair + 1, base)
            scatter_step(pair, base)

        rows_loop(both)
        return carry

    last = cells // 2 - 1
    lax.fori_loop(0, last, pair_step, 0)
    multiply(last)
    rows_loop(lambda base: scatter_step(last, base))

    def total(rows):
        value = accs[0][rows, :]
        for acc in accs[1:]:
            value = value + acc[rows, :]
        return value

    def collect(rows):
        own_ref[rows, :] = total(rows)

    chunks(nodes, 64, collect)
    for part in range(ghosts // 64):
        back_ref[pl.ds(part * 64, 64), :] = total(pl.ds(nodes + part * 64, 64))


def operate(v, ghosts, matrix, maps, scale):
    nodes, columns = v.shape
    count = ghosts.shape[0]
    nc = matrix.shape[0]
    return pl.pallas_call(
        operate_kernel,
        out_shape=(
            jax.ShapeDtypeStruct((nodes, columns), jnp.float32),
            jax.ShapeDtypeStruct((count, columns), jnp.float32),
        ),
        in_specs=[VM, VM, VM, SM, SM],
        out_specs=(VM, VM),
        scratch_shapes=[
            pltpu.VMEM((nodes + count, columns), jnp.float32),
        ]
        + [pltpu.VMEM((nc, columns), jnp.float32)] * 4
        + [pltpu.VMEM((nodes + count, columns), jnp.float32)] * ACCS,
        compiler_params=params(),
        name="operate",
    )(v, ghosts, matrix, maps, scale)


def combine_kernel(first, own_ref, back_ref, v_ref, w_ref, diag_ref, targets_ref, coef_ref, *rest):
    nodes, columns = v_ref.shape
    count = back_ref.shape[0]
    slot = count // 4
    out_ref, accs = rest[0], rest[1:]
    group = 4

    def fill(rows):
        accs[0][rows, :] = own_ref[rows, :]
        for acc in accs[1:]:
            acc[rows, :] = jnp.zeros((64, columns), jnp.float32)

    chunks(nodes, 64, fill)

    def step(i, carry):
        for u in range(group):
            spots = []
            for o in range(4):
                row = i * group + u + o * slot
                at = pl.ds(targets_ref[row], 1)
                spots.append((accs[o], at, accs[o][at, :] + back_ref[pl.ds(row, 1), :]))
            for acc, at, value in spots:
                acc[at, :] = value
        return carry

    lax.fori_loop(0, slot // group, step, 0)
    coef = coef_ref[0]

    def finish(rows):
        total = (accs[0][rows, :] + accs[1][rows, :]) + (accs[2][rows, :] + accs[3][rows, :])
        image = total * coef + diag_ref[rows, :] * v_ref[rows, :].astype(jnp.float32)
        if first:
            value = image.astype(jnp.bfloat16)
        else:
            value = (2.0 * image - w_ref[rows, :].astype(jnp.float32)).astype(jnp.bfloat16)
        out_ref[rows, :] = value

    chunks(nodes, 64, finish)


def combine(first, own, back, v, w, diag, targets, coef):
    nodes, columns = v.shape
    return pl.pallas_call(
        functools.partial(combine_kernel, first),
        out_shape=jax.ShapeDtypeStruct((nodes, columns), jnp.bfloat16),
        in_specs=[VM, VM, VM, VM, VM, SM, SM],
        out_specs=VM,
        scratch_shapes=[pltpu.VMEM((nodes + 8, columns), jnp.float32)] * 4,
        compiler_params=params(),
        name="combine_one" if first else "combine_two",
    )(own, back, v, w, diag, targets, coef)


def margin_kernel(scaling, x_ref, other_ref, margin_ref, part, slots, send_sem, recv_sem):
    columns = x_ref.shape[1]
    nodes = x_ref.shape[0]
    half_rows = columns // 2
    me = lax.axis_index("dom")
    mine = lax.axis_index("band")
    size = lax.axis_size("dom")
    bits = size.bit_length() - 1
    partners = [{"band": 1 - mine}]
    for k in range(bits):
        bit = 1 << k
        partners.append({"dom": me + bit - 2 * bit * (lax.div(me, bit) % 2)})

    barrier = pltpu.get_barrier_semaphore()
    for partner in partners:
        pl.semaphore_signal(barrier, inc=1, device_id=partner, device_id_type=MESH)
    pl.semaphore_wait(barrier, len(partners))

    def send(at, src, dst, partner):
        copy = pltpu.make_async_remote_copy(
            src_ref=src,
            dst_ref=dst,
            send_sem=send_sem.at[at],
            recv_sem=recv_sem.at[at],
            device_id=partner,
            device_id_type=MESH,
        )
        copy.start()
        return copy

    panel = send(0, x_ref, other_ref, partners[0])
    size_k = 512

    def product(right, lanes):
        def step(i, total):
            rows = pl.ds(pl.multiple_of(i * size_k, size_k), size_k)
            return total + lax.dot_general(
                x_ref[rows, :],
                right[rows, :],
                (((0,), (0,)), ((), ())),
                preferred_element_type=jnp.float32,
            )

        part[:, lanes] = lax.fori_loop(
            0, nodes // size_k, step, jnp.zeros((columns, columns), jnp.float32)
        )

    product(x_ref, pl.ds(0, columns))
    panel.wait()
    product(other_ref, pl.ds(columns, columns))

    low = me % 2
    keep = pl.ds(pl.multiple_of(low * half_rows, half_rows), half_rows)
    give = pl.ds(pl.multiple_of((1 - low) * half_rows, half_rows), half_rows)
    copy = send(1, part.at[give], slots.at[0], partners[1])
    copy.wait()
    part[keep, :] += slots[0]
    for k in range(1, bits):
        copy = send(1 + k, part.at[keep], slots.at[k], partners[1 + k])
        copy.wait()
        part[keep, :] += slots[k]
    copy = send(1 + bits, part.at[keep], slots.at[bits], partners[1])
    copy.wait()
    part[give, :] = slots[bits]
    rows_mine = pl.ds(pl.multiple_of(mine * columns, columns), columns)
    lanes_other = pl.ds(pl.multiple_of((1 - mine) * columns, columns), columns)
    margin_ref[rows_mine, rows_mine] = part[:, :columns] * scaling
    margin_ref[rows_mine, lanes_other] = part[:, columns:] * scaling
    copy = send(2 + bits, margin_ref.at[rows_mine], margin_ref.at[rows_mine], partners[0])
    copy.wait()


def margin_of(x, scaling):
    nodes, columns = x.shape
    size = lax.axis_size("dom")
    bits = size.bit_length() - 1
    return pl.pallas_call(
        functools.partial(margin_kernel, scaling),
        out_shape=(
            jax.ShapeDtypeStruct((nodes, columns), x.dtype),
            jax.ShapeDtypeStruct((2 * columns, 2 * columns), jnp.float32),
        ),
        in_specs=[VM],
        out_specs=(VM, VM),
        scratch_shapes=[
            pltpu.VMEM((columns, 2 * columns), jnp.float32),
            pltpu.VMEM((bits + 1, columns // 2, 2 * columns), jnp.float32),
            pltpu.SemaphoreType.DMA((bits + 3,)),
            pltpu.SemaphoreType.DMA((bits + 3,)),
        ],
        compiler_params=params(collective_id=3, has_side_effects=True),
        name="margin",
    )(x)


BLOCK = 64


def inverse_factor(block, spread):
    width = 2 * BLOCK
    shape = (8, width)
    count = BLOCK // 8
    lane = lax.broadcasted_iota(jnp.int32, shape, 1)
    sub = lax.broadcasted_iota(jnp.int32, shape, 0)
    doubled = jnp.concatenate([block, block], 1)
    tiles = []
    for t in range(count):
        unit = (lane - BLOCK == sub + 8 * t).astype(jnp.float32)
        tiles.append(jnp.where(lane < BLOCK, doubled[8 * t : 8 * t + 8], unit))
    done = []
    for g in range(count):
        here = spread.at[g % 2]
        for k in range(8):
            here[8 * k : 8 * k + 8, :] = jnp.broadcast_to(tiles[g][:, 8 * g + k : 8 * g + k + 1], shape)
        here[64:72, :] = tiles[g]

        def replicated(at):
            return jnp.broadcast_to(here[at : at + 1, :], shape)

        a = [[replicated(8 * k + i) for k in range(i + 1)] for i in range(8)]
        rows = [replicated(64 + i) for i in range(8)]
        recip = []
        for k in range(8):
            recip.append(1.0 / a[k][k])
            scaled = {i: a[i][k] * recip[k] for i in range(k + 1, 8)}
            for i in range(k + 1, 8):
                for l in range(k + 1, i + 1):
                    a[i][l] = a[i][l] - scaled[i] * a[l][k]
            for i in range(k + 1, 8):
                rows[i] = rows[i] - scaled[i] * rows[k]
                a[i][k] = scaled[i]
        whole = rows[0] * lax.rsqrt(a[0][0])
        for i in range(1, 8):
            whole = jnp.where(sub == i, rows[i] * lax.rsqrt(a[i][i]), whole)
        done.append(whole)
        if g + 1 == count:
            break
        solved = [None] * 8
        for i in range(7, -1, -1):
            value = rows[i] * recip[i]
            for l in range(7, i, -1):
                value = value - a[l][i] * solved[l]
            solved[i] = value
        for t in range(g + 1, count):
            parts = [
                jnp.broadcast_to(tiles[t][:, 8 * g + k : 8 * g + k + 1], shape) * solved[k]
                for k in range(8)
            ]
            while len(parts) > 1:
                parts = [parts[n] + parts[n + 1] for n in range(0, len(parts), 2)]
            tiles[t] = tiles[t] - parts[0]
    return jnp.concatenate(done, 0)[:, BLOCK:]


def finish_kernel(margin_ref, x_ref, other_ref, mine_ref, out_ref, work, spread):
    nodes, columns = x_ref.shape
    bands = margin_ref.shape[0]
    exact = lax.Precision.HIGHEST
    work[...] = margin_ref[...]
    for first in range(0, bands, BLOCK):
        last = first + BLOCK
        inverse = inverse_factor(work[first:last, first:last], spread)
        pieces = [inverse]
        if first:
            pieces = [work[first:last, :first]] + pieces
        if last < bands:
            pieces = pieces + [work[first:last, last:]]
        for at, piece in enumerate(pieces):
            if piece is not inverse:
                pieces[at] = jnp.dot(inverse, piece, precision=exact)
        row = jnp.concatenate(pieces, 1) if len(pieces) > 1 else pieces[0]
        lane = lax.broadcasted_iota(jnp.int32, (BLOCK, bands), 1)
        work[first:last, :] = jnp.where(lane < last, row, 0.0)
        if last < bands:
            update = lax.dot_general(
                row[:, last:], row, (((0,), (0,)), ((), ())), precision=exact
            )
            lane = lax.broadcasted_iota(jnp.int32, (bands - last, bands), 1)
            fresh = jnp.logical_and(lane >= first, lane < last)
            work[last:, :] = jnp.where(fresh, 0.0, work[last:, :]) - update

    mine = mine_ref[0]
    own_at = pl.ds(pl.multiple_of(mine * columns, columns), columns)
    other_at = pl.ds(pl.multiple_of((1 - mine) * columns, columns), columns)
    rows = jnp.concatenate([work[own_at, own_at], work[own_at, other_at]], 1)
    high = rows.astype(jnp.bfloat16)
    low = (rows - high.astype(jnp.float32)).astype(jnp.bfloat16)
    both = jnp.concatenate([high, low], 0)

    def rotate(at):
        panel = jnp.concatenate([x_ref[at, :], other_ref[at, :]], 1)
        value = lax.dot_general(
            panel, both, (((1,), (1,)), ((), ())), preferred_element_type=jnp.float32
        )
        out_ref[at, :] = value[:, :columns] + value[:, columns:]

    chunks(nodes, 512, rotate)


def finish(margin, x, other, mine):
    return pl.pallas_call(
        finish_kernel,
        out_shape=jax.ShapeDtypeStruct(x.shape, jnp.float32),
        in_specs=[VM, VM, VM, SM],
        out_specs=VM,
        scratch_shapes=[
            pltpu.VMEM(margin.shape, jnp.float32),
            pltpu.VMEM((2, 72, 2 * BLOCK), jnp.float32),
        ],
        compiler_params=params(),
        name="finish",
    )(margin, x, other, mine)


def on_device(wavefunctions, bounds, cell_matrix, cell_scale, potential, cell_nodes, face_nodes):
    nodes, columns = wavefunctions.shape
    targets = jnp.where(face_nodes >= 0, face_nodes, nodes).reshape(-1)
    maps = cell_nodes.reshape(-1)
    center = (bounds[0] + bounds[1]) / 2.0
    coef = 1.0 / ((bounds[1] - bounds[0]) / 2.0)
    diag = jnp.broadcast_to(((potential - center) * coef)[:, None], (nodes, columns))
    coef = coef.reshape(1)

    def apply_sums(vectors):
        ghosts = exchange_out(vectors, targets)
        own, back = operate(vectors, ghosts, cell_matrix, maps, cell_scale)
        return own, exchange_back(back)

    own, back = apply_sums(wavefunctions)
    one = combine(True, own, back, wavefunctions, wavefunctions, diag, targets, coef)
    own, back = apply_sums(one)
    two = combine(False, own, back, one, wavefunctions, diag, targets, coef)
    other, margin = margin_of(two, 1.0 / (nodes * lax.axis_size("dom")))
    return finish(margin, two, other, lax.axis_index("band").reshape(1))


def solution(mesh):
    return jax.shard_map(
        on_device,
        mesh=mesh,
        in_specs=(
            P(("kpt", "dom"), "band"),
            P("kpt"),
            P(),
            P("dom"),
            P("dom"),
            P("dom", None),
            P("dom", None),
        ),
        out_specs=P(("kpt", "dom"), "band"),
        check_vma=False,
    )
```

```python
import functools

import jax
import jax.numpy as jnp
from jax import lax
from jax.experimental import pallas as pl
from jax.experimental.pallas import tpu as pltpu
from jax.sharding import PartitionSpec as P

peer_offsets = (1, -1, 2, -2)
MESH = pl.DeviceIdType.MESH
VM = pl.BlockSpec(memory_space=pltpu.VMEM)
SM = pl.BlockSpec(memory_space=pltpu.SMEM)
ACCS = 8


def params(mib=20, **more):
    return pltpu.CompilerParams(vmem_limit_bytes=mib * 1024 * 1024, **more)


def chunks(total, size, body):
    def step(i, carry):
        body(pl.ds(pl.multiple_of(i * size, size), size))
        return carry

    lax.fori_loop(0, total // size, step, 0)


def exists(by):
    there = lax.axis_index("dom") + by
    return jnp.logical_and(there >= 0, there < lax.axis_size("dom"))


def greet_neighbours(barrier):
    me = lax.axis_index("dom")
    for by in peer_offsets:

        @pl.when(exists(by))
        def _():
            pl.semaphore_signal(
                barrier, inc=1, device_id={"dom": me + by}, device_id_type=MESH
            )


def await_neighbours(barrier):
    peers = jnp.int32(0)
    for by in peer_offsets:
        peers = peers + exists(by).astype(jnp.int32)
    pl.semaphore_wait(barrier, peers)


def face_copy(sign, o, send_ref, recv_ref, send_sem, recv_sem):
    rows = pl.ds(o * (send_ref.shape[0] // 4), send_ref.shape[0] // 4)
    return pltpu.make_async_remote_copy(
        src_ref=send_ref.at[rows],
        dst_ref=recv_ref.at[rows],
        send_sem=send_sem.at[o],
        recv_sem=recv_sem.at[o],
        device_id={"dom": lax.axis_index("dom") + sign * peer_offsets[o]},
        device_id_type=MESH,
    )


def start_face(sign, o, *refs):
    @pl.when(exists(sign * peer_offsets[o]))
    def _():
        face_copy(sign, o, *refs).start()


def end_faces(sign, *refs):
    recv_ref = refs[1]
    slot = recv_ref.shape[0] // 4
    for o in range(4):

        @pl.when(jnp.logical_not(exists(-sign * peer_offsets[o])))
        def _():
            recv_ref[pl.ds(o * slot, slot), :] = jnp.zeros(
                (slot, recv_ref.shape[1]), recv_ref.dtype
            )

    for o in range(4):

        @pl.when(exists(sign * peer_offsets[o]))
        def _():
            face_copy(sign, o, *refs).wait_send()

        @pl.when(exists(-sign * peer_offsets[o]))
        def _():
            face_copy(sign, o, *refs).wait_recv()


def back_kernel(send_ref, recv_ref, send_sem, recv_sem):
    refs = (send_ref, recv_ref, send_sem, recv_sem)
    barrier = pltpu.get_barrier_semaphore()
    greet_neighbours(barrier)
    await_neighbours(barrier)
    for o in (2, 3, 0, 1):
        start_face(-1, o, *refs)
    end_faces(-1, *refs)


def exchange_back(values):
    return pl.pallas_call(
        back_kernel,
        out_shape=jax.ShapeDtypeStruct(values.shape, values.dtype),
        in_specs=[VM],
        out_specs=VM,
        scratch_shapes=[pltpu.SemaphoreType.DMA((4,)), pltpu.SemaphoreType.DMA((4,))],
        compiler_params=params(collective_id=2, has_side_effects=True),
        name="exchange_back",
    )(values)


def out_kernel(v_ref, targets_ref, recv_ref, wide, stage, send, send_sem, recv_sem):
    nodes, columns = v_ref.shape
    slot = send.shape[0] // 4
    group = 16
    refs = (send, recv_ref, send_sem, recv_sem)
    barrier = pltpu.get_barrier_semaphore()
    greet_neighbours(barrier)

    def widen(rows):
        wide[rows, :] = v_ref[rows, :].astype(jnp.float32)

    chunks(nodes, 256, widen)
    wide[pl.ds(nodes, 8), :] = jnp.zeros((8, columns), jnp.float32)
    order = (0, 1, 2, 3)
    for o in order:

        def step(i, carry):
            base = pl.multiple_of(o * slot + i * group, group)
            rows = [wide[pl.ds(targets_ref[base + u], 1), :] for u in range(group)]
            for u in range(group):
                stage[pl.ds(base + u, 1), :] = rows[u]
            return carry

        lax.fori_loop(0, slot // group, step, 0)
        rows = pl.ds(o * slot, slot)
        send[rows, :] = stage[rows, :].astype(send.dtype)
        if o == order[0]:
            await_neighbours(barrier)
        start_face(1, o, *refs)
    end_faces(1, *refs)


def exchange_out(v, targets):
    nodes, columns = v.shape
    count = targets.shape[0]
    return pl.pallas_call(
        out_kernel,
        out_shape=jax.ShapeDtypeStruct((count, columns), v.dtype),
        in_specs=[VM, SM],
        out_specs=VM,
        scratch_shapes=[
            pltpu.VMEM((nodes + 8, columns), jnp.float32),
            pltpu.VMEM((count, columns), jnp.float32),
            pltpu.VMEM((count, columns), v.dtype),
            pltpu.SemaphoreType.DMA((4,)),
            pltpu.SemaphoreType.DMA((4,)),
        ],
        compiler_params=params(collective_id=1, has_side_effects=True),
        name="exchange_out",
    )(v, targets)


def operate_kernel(
    v_ref, ghost_ref, matrix_ref, maps_ref, scale_ref, own_ref, back_ref, ext, *rest
):
    nodes, columns = v_ref.shape
    ghosts = ghost_ref.shape[0]
    nc = matrix_ref.shape[0]
    cells = scale_ref.shape[0]
    group = 32
    gat, prod, accs = rest[:2], rest[2:4], rest[4:]

    def widen(rows):
        ext[rows, :] = v_ref[rows, :].astype(jnp.float32)

    chunks(nodes, 256, widen)
    for part in range(ghosts // 256):
        ext[pl.ds(nodes + part * 256, 256), :] = ghost_ref[pl.ds(part * 256, 256), :].astype(
            jnp.float32
        )

    def clear(rows):
        for acc in accs:
            acc[rows, :] = jnp.zeros((64, columns), jnp.float32)

    chunks(nodes + ghosts, 64, clear)

    def gather_step(pair, base):
        rows = [
            (u, h, ext[pl.ds(maps_ref[(2 * pair + h) * nc + base + u], 1), :])
            for u in range(ACCS // 2)
            for h in range(2)
        ]
        for u, h, row in rows:
            gat[h][pl.ds(base + u, 1), :] = row

    def scatter_step(pair, base):
        spots = []
        for u in range(ACCS // 2):
            for h in range(2):
                at = pl.ds(maps_ref[(2 * pair + h) * nc + base + u], 1)
                acc = accs[2 * u + h]
                spots.append((acc, at, acc[at, :] + prod[h][pl.ds(base + u, 1), :]))
        for acc, at, value in spots:
            acc[at, :] = value

    def rows_loop(body):
        def step(i, carry):
            base = pl.multiple_of(i * group, group)
            for first in range(0, group, ACCS // 2):
                body(base + first)
            return carry

        lax.fori_loop(0, nc // group, step, 0)

    def multiply(pair):
        both = jnp.concatenate([gat[0][...], gat[1][...]], 1).astype(jnp.bfloat16)
        result = jnp.dot(matrix_ref[...], both, preferred_element_type=jnp.float32)
        for h in range(2):
            prod[h][...] = (
                result[:, h * columns : (h + 1) * columns] * scale_ref[2 * pair + h]
            )

    rows_loop(lambda base: gather_step(0, base))

    def pair_step(pair, carry):
        multiply(pair)

        def both(base):
            gather_step(pair + 1, base)
            scatter_step(pair, base)

        rows_loop(both)
        return carry

    last = cells // 2 - 1
    lax.fori_loop(0, last, pair_step, 0)
    multiply(last)
    rows_loop(lambda base: scatter_step(last, base))

    def total(rows):
        value = accs[0][rows, :]
        for acc in accs[1:]:
            value = value + acc[rows, :]
        return value

    def collect(rows):
        own_ref[rows, :] = total(rows)

    chunks(nodes, 64, collect)
    for part in range(ghosts // 64):
        back_ref[pl.ds(part * 64, 64), :] = total(pl.ds(nodes + part * 64, 64))


def operate(v, ghosts, matrix, maps, scale):
    nodes, columns = v.shape
    count = ghosts.shape[0]
    nc = matrix.shape[0]
    return pl.pallas_call(
        operate_kernel,
        out_shape=(
            jax.ShapeDtypeStruct((nodes, columns), jnp.float32),
            jax.ShapeDtypeStruct((count, columns), jnp.float32),
        ),
        in_specs=[VM, VM, VM, SM, SM],
        out_specs=(VM, VM),
        scratch_shapes=[
            pltpu.VMEM((nodes + count, columns), jnp.float32),
        ]
        + [pltpu.VMEM((nc, columns), jnp.float32)] * 4
        + [pltpu.VMEM((nodes + count, columns), jnp.float32)] * ACCS,
        compiler_params=params(36),
        name="operate",
    )(v, ghosts, matrix, maps, scale)


def combine_kernel(first, own_ref, back_ref, v_ref, w_ref, potential_ref, targets_ref, bounds_ref, *rest):
    nodes, columns = v_ref.shape
    count = back_ref.shape[0]
    slot = count // 4
    out_ref, accs = rest[0], rest[1:]
    group = 4

    def fill(rows):
        accs[0][rows, :] = own_ref[rows, :]
        for acc in accs[1:]:
            acc[rows, :] = jnp.zeros((64, columns), jnp.float32)

    chunks(nodes, 64, fill)

    def step(i, carry):
        for u in range(group):
            spots = []
            for o in range(4):
                row = i * group + u + o * slot
                at = pl.ds(targets_ref[row], 1)
                spots.append((accs[o], at, accs[o][at, :] + back_ref[pl.ds(row, 1), :]))
            for acc, at, value in spots:
                acc[at, :] = value
        return carry

    lax.fori_loop(0, slot // group, step, 0)
    center = (bounds_ref[0] + bounds_ref[1]) * 0.5
    coef = 1.0 / jnp.full((1, columns), (bounds_ref[1] - bounds_ref[0]) * 0.5, jnp.float32)
    size = potential_ref.shape[1]
    turned = potential_ref[...].T - center
    for i in range(nodes // size):
        rows = pl.ds(i * size, size)
        total = (accs[0][rows, :] + accs[1][rows, :]) + (accs[2][rows, :] + accs[3][rows, :])
        level = jnp.broadcast_to(turned[:, i : i + 1], (size, columns))
        image = (total + level * v_ref[rows, :].astype(jnp.float32)) * coef
        if not first:
            image = 2.0 * image - w_ref[rows, :].astype(jnp.float32)
        out_ref[rows, :] = image.astype(jnp.bfloat16)


def combine(first, own, back, v, w, potential, targets, bounds):
    nodes, columns = v.shape
    return pl.pallas_call(
        functools.partial(combine_kernel, first),
        out_shape=jax.ShapeDtypeStruct((nodes, columns), jnp.bfloat16),
        in_specs=[VM, VM, VM, VM, VM, SM, SM],
        out_specs=VM,
        scratch_shapes=[pltpu.VMEM((nodes + 8, columns), jnp.float32)] * 4,
        compiler_params=params(),
        name="combine_one" if first else "combine_two",
    )(own, back, v, w, potential, targets, bounds)


PIECES = 4


def margin_kernel(scaling, x_ref, other_ref, margin_ref, part, slots, send_sem, recv_sem):
    nodes, columns = x_ref.shape
    me = lax.axis_index("dom")
    mine = lax.axis_index("band")
    size = lax.axis_size("dom")
    across = {"band": 1 - mine}
    direct = columns // size >= 8
    if direct:
        peers = [{"dom": lax.rem(me + by, size)} for by in range(1, size)]
    else:
        peers = []
        for k in range(size.bit_length() - 1):
            bit = 1 << k
            peers.append({"dom": me + bit - 2 * bit * (lax.div(me, bit) % 2)})

    barrier = pltpu.get_barrier_semaphore()
    for peer in [across] + peers:
        pl.semaphore_signal(barrier, inc=1, device_id=peer, device_id_type=MESH)
    pl.semaphore_wait(barrier, 1 + len(peers))

    def send(at, src, dst, peer):
        copy = pltpu.make_async_remote_copy(
            src_ref=src,
            dst_ref=dst,
            send_sem=send_sem.at[at],
            recv_sem=recv_sem.at[at],
            device_id=peer,
            device_id_type=MESH,
        )
        copy.start()
        return copy

    chunk = nodes // PIECES
    copies = []
    for c in range(PIECES):
        rows = pl.ds(c * chunk, chunk)
        copies.append(send(c, x_ref.at[rows], other_ref.at[rows], across))
    sums = jnp.zeros((columns, 2 * columns), jnp.float32)
    for c in range(PIECES):
        copies[c].wait()

        def step(i, total):
            rows = pl.ds(pl.multiple_of(c * chunk + i * 256, 256), 256)
            own = x_ref[rows, :]
            return total + lax.dot_general(
                own,
                jnp.concatenate([own, other_ref[rows, :]], 1),
                (((0,), (0,)), ((), ())),
                preferred_element_type=jnp.float32,
            )

        sums = lax.fori_loop(0, chunk // 256, step, sums)
    sums = sums * scaling
    lanes_mine = pl.ds(pl.multiple_of(mine * columns, columns), columns)
    lanes_other = pl.ds(pl.multiple_of((1 - mine) * columns, columns), columns)
    part[:, lanes_mine] = sums[:, :columns]
    part[:, lanes_other] = sums[:, columns:]
    at = PIECES

    if direct:
        piece = columns // size

        def rows_of(owner):
            return pl.ds(pl.multiple_of(owner * piece, piece), piece)

        def margin_rows(owner):
            return pl.ds(pl.multiple_of(mine * columns + owner * piece, piece), piece)

        copies = []
        for by in range(1, size):
            to = lax.rem(me + by, size)
            copies.append(send(at + by, part.at[rows_of(to)], slots.at[by], peers[by - 1]))
        total = part[rows_of(me), :]
        for by in range(1, size):
            copies[by - 1].wait()
            total = total + slots[by]
        margin_ref[margin_rows(me), :] = total
        at = at + size
        home = margin_ref.at[margin_rows(me)]
        copies = [send(at + by, home, home, peers[by - 1]) for by in range(1, size)]
        at = at + size
        forwards = [send(at, home, home, across)]
        for by in range(1, size):
            copies[by - 1].wait()
            came = margin_ref.at[margin_rows(lax.rem(me + size - by, size))]
            forwards.append(send(at + by, came, came, across))
        for copy in forwards:
            copy.wait()
    else:
        for k, peer in enumerate(peers):
            copy = send(at + k, part, slots.at[k], peer)
            copy.wait()
            part[...] += slots[k]
        margin_ref[lanes_mine, :] = part[...]
        home = margin_ref.at[lanes_mine]
        send(at + len(peers), home, home, across).wait()


def margin_of(x, scaling):
    nodes, columns = x.shape
    size = lax.axis_size("dom")
    direct = columns // size >= 8
    slots = (size, columns // size) if direct else (size.bit_length(), columns)
    copies = PIECES + (3 * size if direct else size.bit_length() + 1)
    return pl.pallas_call(
        functools.partial(margin_kernel, scaling),
        out_shape=(
            jax.ShapeDtypeStruct((nodes, columns), x.dtype),
            jax.ShapeDtypeStruct((2 * columns, 2 * columns), jnp.float32),
        ),
        in_specs=[VM],
        out_specs=(VM, VM),
        scratch_shapes=[
            pltpu.VMEM((columns, 2 * columns), jnp.float32),
            pltpu.VMEM(slots + (2 * columns,), jnp.float32),
            pltpu.SemaphoreType.DMA((copies,)),
            pltpu.SemaphoreType.DMA((copies,)),
        ],
        compiler_params=params(collective_id=3, has_side_effects=True),
        name="margin",
    )(x)


BLOCK = 64


def inverse_factor(block, spread):
    width = 2 * BLOCK
    shape = (8, width)
    count = BLOCK // 8
    lane = lax.broadcasted_iota(jnp.int32, shape, 1)
    sub = lax.broadcasted_iota(jnp.int32, shape, 0)
    doubled = jnp.concatenate([block, block], 1)
    tiles = []
    for t in range(count):
        unit = (lane - BLOCK == sub + 8 * t).astype(jnp.float32)
        tiles.append(jnp.where(lane < BLOCK, doubled[8 * t : 8 * t + 8], unit))
    done = []
    for g in range(count):
        here = spread.at[g % 2]
        for k in range(8):
            here[8 * k : 8 * k + 8, :] = jnp.broadcast_to(tiles[g][:, 8 * g + k : 8 * g + k + 1], shape)
        here[64:72, :] = tiles[g]

        def replicated(at):
            return jnp.broadcast_to(here[at : at + 1, :], shape)

        a = [[replicated(8 * k + i) for k in range(i + 1)] for i in range(8)]
        rows = [replicated(64 + i) for i in range(8)]
        recip = []
        for k in range(8):
            recip.append(1.0 / a[k][k])
            scaled = {i: a[i][k] * recip[k] for i in range(k + 1, 8)}
            for i in range(k + 1, 8):
                for l in range(k + 1, i + 1):
                    a[i][l] = a[i][l] - scaled[i] * a[l][k]
            for i in range(k + 1, 8):
                rows[i] = rows[i] - scaled[i] * rows[k]
                a[i][k] = scaled[i]
        whole = rows[0] * lax.rsqrt(a[0][0])
        for i in range(1, 8):
            whole = jnp.where(sub == i, rows[i] * lax.rsqrt(a[i][i]), whole)
        done.append(whole)
        if g + 1 == count:
            break
        solved = [None] * 8
        for i in range(7, -1, -1):
            value = rows[i] * recip[i]
            for l in range(7, i, -1):
                value = value - a[l][i] * solved[l]
            solved[i] = value
        for t in range(g + 1, count):
            parts = [
                jnp.broadcast_to(tiles[t][:, 8 * g + k : 8 * g + k + 1], shape) * solved[k]
                for k in range(8)
            ]
            while len(parts) > 1:
                parts = [parts[n] + parts[n + 1] for n in range(0, len(parts), 2)]
            tiles[t] = tiles[t] - parts[0]
    return jnp.concatenate(done, 0)[:, BLOCK:]


def finish_kernel(margin_ref, x_ref, other_ref, mine_ref, out_ref, work, spread):
    nodes, columns = x_ref.shape
    bands = margin_ref.shape[0]
    exact = lax.Precision.HIGHEST
    work[...] = margin_ref[...]
    for first in range(0, bands, BLOCK):
        last = first + BLOCK
        inverse = inverse_factor(work[first:last, first:last], spread)
        pieces = [inverse]
        if first:
            pieces = [work[first:last, :first]] + pieces
        if last < bands:
            pieces = pieces + [work[first:last, last:]]
        for at, piece in enumerate(pieces):
            if piece is not inverse:
                pieces[at] = jnp.dot(inverse, piece, precision=exact)
        row = jnp.concatenate(pieces, 1) if len(pieces) > 1 else pieces[0]
        lane = lax.broadcasted_iota(jnp.int32, (BLOCK, bands), 1)
        work[first:last, :] = jnp.where(lane < last, row, 0.0)
        if last < bands:
            update = lax.dot_general(
                row[:, last:], row, (((0,), (0,)), ((), ())), precision=exact
            )
            lane = lax.broadcasted_iota(jnp.int32, (bands - last, bands), 1)
            fresh = jnp.logical_and(lane >= first, lane < last)
            work[last:, :] = jnp.where(fresh, 0.0, work[last:, :]) - update

    mine = mine_ref[0]
    own_at = pl.ds(pl.multiple_of(mine * columns, columns), columns)
    other_at = pl.ds(pl.multiple_of((1 - mine) * columns, columns), columns)
    rows = jnp.concatenate([work[own_at, own_at], work[own_at, other_at]], 1)
    high = rows.astype(jnp.bfloat16)
    low = (rows - high.astype(jnp.float32)).astype(jnp.bfloat16)
    both = jnp.concatenate([high, low], 0)

    def rotate(at):
        panel = jnp.concatenate([x_ref[at, :], other_ref[at, :]], 1)
        value = lax.dot_general(
            panel, both, (((1,), (1,)), ((), ())), preferred_element_type=jnp.float32
        )
        out_ref[at, :] = value[:, :columns] + value[:, columns:]

    chunks(nodes, 512, rotate)


def finish(margin, x, other, mine):
    return pl.pallas_call(
        finish_kernel,
        out_shape=jax.ShapeDtypeStruct(x.shape, jnp.float32),
        in_specs=[VM, VM, VM, SM],
        out_specs=VM,
        scratch_shapes=[
            pltpu.VMEM(margin.shape, jnp.float32),
            pltpu.VMEM((2, 72, 2 * BLOCK), jnp.float32),
        ],
        compiler_params=params(),
        name="finish",
    )(margin, x, other, mine)


def on_device(wavefunctions, bounds, cell_matrix, cell_scale, potential, cell_nodes, face_nodes):
    nodes, columns = wavefunctions.shape
    targets = jnp.where(face_nodes >= 0, face_nodes, nodes).reshape(-1)
    maps = cell_nodes.reshape(-1)
    levels = potential.reshape(nodes // 128, 128)

    def apply_sums(vectors):
        ghosts = exchange_out(vectors, targets)
        own, back = operate(vectors, ghosts, cell_matrix, maps, cell_scale)
        return own, exchange_back(back)

    own, back = apply_sums(wavefunctions)
    one = combine(True, own, back, wavefunctions, wavefunctions, levels, targets, bounds)
    own, back = apply_sums(one)
    two = combine(False, own, back, one, wavefunctions, levels, targets, bounds)
    other, margin = margin_of(two, 1.0 / (nodes * lax.axis_size("dom")))
    return finish(margin, two, other, lax.axis_index("band").reshape(1))


def solution(mesh):
    return jax.shard_map(
        on_device,
        mesh=mesh,
        in_specs=(
            P(("kpt", "dom"), "band"),
            P("kpt"),
            P(),
            P("dom"),
            P("dom"),
            P("dom", None),
            P("dom", None),
        ),
        out_specs=P(("kpt", "dom"), "band"),
        check_vma=False,
    )
```

```python
import functools

import jax
import jax.numpy as jnp
from jax import lax
from jax.experimental import pallas as pl
from jax.experimental.pallas import tpu as pltpu
from jax.sharding import PartitionSpec as P

peer_offsets = (1, -1, 2, -2)
MESH = pl.DeviceIdType.MESH
VM = pl.BlockSpec(memory_space=pltpu.VMEM)
SM = pl.BlockSpec(memory_space=pltpu.SMEM)
ACCS = 8


def params(mib=20, **more):
    return pltpu.CompilerParams(vmem_limit_bytes=mib * 1024 * 1024, **more)


def chunks(total, size, body):
    def step(i, carry):
        body(pl.ds(pl.multiple_of(i * size, size), size))
        return carry

    lax.fori_loop(0, total // size, step, 0)


def exists(by):
    there = lax.axis_index("dom") + by
    return jnp.logical_and(there >= 0, there < lax.axis_size("dom"))


def greet_neighbours(barrier):
    me = lax.axis_index("dom")
    for by in peer_offsets:

        @pl.when(exists(by))
        def _():
            pl.semaphore_signal(
                barrier, inc=1, device_id={"dom": me + by}, device_id_type=MESH
            )


def await_neighbours(barrier):
    peers = jnp.int32(0)
    for by in peer_offsets:
        peers = peers + exists(by).astype(jnp.int32)
    pl.semaphore_wait(barrier, peers)


def face_copy(sign, o, send_ref, recv_ref, send_sem, recv_sem):
    rows = pl.ds(o * (send_ref.shape[0] // 4), send_ref.shape[0] // 4)
    return pltpu.make_async_remote_copy(
        src_ref=send_ref.at[rows],
        dst_ref=recv_ref.at[rows],
        send_sem=send_sem.at[o],
        recv_sem=recv_sem.at[o],
        device_id={"dom": lax.axis_index("dom") + sign * peer_offsets[o]},
        device_id_type=MESH,
    )


def start_face(sign, o, *refs):
    @pl.when(exists(sign * peer_offsets[o]))
    def _():
        face_copy(sign, o, *refs).start()


def end_faces(sign, *refs):
    recv_ref = refs[1]
    slot = recv_ref.shape[0] // 4
    for o in range(4):

        @pl.when(jnp.logical_not(exists(-sign * peer_offsets[o])))
        def _():
            recv_ref[pl.ds(o * slot, slot), :] = jnp.zeros(
                (slot, recv_ref.shape[1]), recv_ref.dtype
            )

    for o in range(4):

        @pl.when(exists(sign * peer_offsets[o]))
        def _():
            face_copy(sign, o, *refs).wait_send()

        @pl.when(exists(-sign * peer_offsets[o]))
        def _():
            face_copy(sign, o, *refs).wait_recv()


def back_kernel(send_ref, recv_ref, send_sem, recv_sem):
    refs = (send_ref, recv_ref, send_sem, recv_sem)
    barrier = pltpu.get_barrier_semaphore()
    greet_neighbours(barrier)
    await_neighbours(barrier)
    for o in (2, 3, 0, 1):
        start_face(-1, o, *refs)
    end_faces(-1, *refs)


def exchange_back(values):
    return pl.pallas_call(
        back_kernel,
        out_shape=jax.ShapeDtypeStruct(values.shape, values.dtype),
        in_specs=[VM],
        out_specs=VM,
        scratch_shapes=[pltpu.SemaphoreType.DMA((4,)), pltpu.SemaphoreType.DMA((4,))],
        compiler_params=params(collective_id=2, has_side_effects=True),
        name="exchange_back",
    )(values)


def out_kernel(v_ref, targets_ref, recv_ref, wide, stage, send, send_sem, recv_sem):
    nodes, columns = v_ref.shape
    slot = send.shape[0] // 4
    group = 16
    refs = (send, recv_ref, send_sem, recv_sem)
    barrier = pltpu.get_barrier_semaphore()
    greet_neighbours(barrier)

    def widen(rows):
        wide[rows, :] = v_ref[rows, :].astype(jnp.float32)

    chunks(nodes, 256, widen)
    wide[pl.ds(nodes, 8), :] = jnp.zeros((8, columns), jnp.float32)
    order = (0, 1, 2, 3)
    for o in order:

        def step(i, carry):
            base = pl.multiple_of(o * slot + i * group, group)
            rows = [wide[pl.ds(targets_ref[base + u], 1), :] for u in range(group)]
            for u in range(group):
                stage[pl.ds(base + u, 1), :] = rows[u]
            return carry

        lax.fori_loop(0, slot // group, step, 0)
        rows = pl.ds(o * slot, slot)
        send[rows, :] = stage[rows, :].astype(send.dtype)
        if o == order[0]:
            await_neighbours(barrier)
        start_face(1, o, *refs)
    end_faces(1, *refs)


def exchange_out(v, targets):
    nodes, columns = v.shape
    count = targets.shape[0]
    return pl.pallas_call(
        out_kernel,
        out_shape=jax.ShapeDtypeStruct((count, columns), v.dtype),
        in_specs=[VM, SM],
        out_specs=VM,
        scratch_shapes=[
            pltpu.VMEM((nodes + 8, columns), jnp.float32),
            pltpu.VMEM((count, columns), jnp.float32),
            pltpu.VMEM((count, columns), v.dtype),
            pltpu.SemaphoreType.DMA((4,)),
            pltpu.SemaphoreType.DMA((4,)),
        ],
        compiler_params=params(collective_id=1, has_side_effects=True),
        name="exchange_out",
    )(v, targets)


def operate_kernel(
    v_ref, ghost_ref, matrix_ref, maps_ref, scale_ref, own_ref, back_ref, ext, *rest
):
    nodes, columns = v_ref.shape
    ghosts = ghost_ref.shape[0]
    nc = matrix_ref.shape[0]
    cells = scale_ref.shape[0]
    group = 64
    gat, prods, both, accs = rest[:2], (rest[2:4], rest[4:6]), rest[6], rest[7:]

    def widen(rows):
        ext[rows, :] = v_ref[rows, :].astype(jnp.float32)

    chunks(nodes, 256, widen)
    for part in range(ghosts // 256):
        ext[pl.ds(nodes + part * 256, 256), :] = ghost_ref[pl.ds(part * 256, 256), :].astype(
            jnp.float32
        )

    def clear(rows):
        for acc in accs:
            acc[rows, :] = jnp.zeros((64, columns), jnp.float32)

    chunks(nodes + ghosts, 64, clear)

    def gather_step(pair, base):
        rows = [
            (u, h, ext[pl.ds(maps_ref[(2 * pair + h) * nc + base + u], 1), :])
            for u in range(ACCS // 2)
            for h in range(2)
        ]
        for u, h, row in rows:
            gat[h][pl.ds(base + u, 1), :] = row

    def scatter_step(pair, base):
        prod = prods[pair % 2]
        spots = []
        for u in range(ACCS // 2):
            for h in range(2):
                at = pl.ds(maps_ref[(2 * pair + h) * nc + base + u], 1)
                acc = accs[2 * u + h]
                spots.append((acc, at, acc[at, :] + prod[h][pl.ds(base + u, 1), :]))
        for acc, at, value in spots:
            acc[at, :] = value

    def multiply(pair, base):
        rows = pl.ds(base, group)
        result = jnp.dot(matrix_ref[rows, :], both[...], preferred_element_type=jnp.float32)
        for h in range(2):
            prods[pair % 2][h][rows, :] = (
                result[:, h * columns : (h + 1) * columns] * scale_ref[2 * pair + h]
            )

    pairs = cells // 2
    for stage in range(pairs + 2):
        gathers = stage < pairs
        multiplies = 0 <= stage - 1 < pairs
        scatters = 0 <= stage - 2 < pairs
        if multiplies:
            for h in range(2):
                both[:, h * columns : (h + 1) * columns] = gat[h][...].astype(both.dtype)

        def step(i, carry):
            base = pl.multiple_of(i * group, group)
            if multiplies:
                multiply(stage - 1, base)
            for first in range(0, group, ACCS // 2):
                if gathers:
                    gather_step(stage, base + first)
                if scatters:
                    scatter_step(stage - 2, base + first)
            return carry

        lax.fori_loop(0, nc // group, step, 0)

    def total(rows):
        value = accs[0][rows, :]
        for acc in accs[1:]:
            value = value + acc[rows, :]
        return value

    def collect(rows):
        own_ref[rows, :] = total(rows)

    chunks(nodes, 64, collect)
    for part in range(ghosts // 64):
        back_ref[pl.ds(part * 64, 64), :] = total(pl.ds(nodes + part * 64, 64)).astype(
            back_ref.dtype
        )


def operate(v, ghosts, matrix, maps, scale):
    nodes, columns = v.shape
    count = ghosts.shape[0]
    nc = matrix.shape[0]
    return pl.pallas_call(
        operate_kernel,
        out_shape=(
            jax.ShapeDtypeStruct((nodes, columns), jnp.float32),
            jax.ShapeDtypeStruct((count, columns), jnp.float32),
        ),
        in_specs=[VM, VM, VM, SM, SM],
        out_specs=(VM, VM),
        scratch_shapes=[
            pltpu.VMEM((nodes + count, columns), jnp.float32),
        ]
        + [pltpu.VMEM((nc, columns), jnp.float32)] * 6
        + [pltpu.VMEM((nc, 2 * columns), matrix.dtype)]
        + [pltpu.VMEM((nodes + count, columns), jnp.float32)] * ACCS,
        compiler_params=params(36),
        name="operate",
    )(v, ghosts, matrix, maps, scale)


def combine_kernel(first, own_ref, back_ref, v_ref, w_ref, potential_ref, targets_ref, bounds_ref, *rest):
    nodes, columns = v_ref.shape
    count = back_ref.shape[0]
    slot = count // 4
    out_ref, wide, accs = rest[0], rest[1], rest[2:]
    wide[...] = back_ref[...].astype(jnp.float32)
    group = 4

    def fill(rows):
        accs[0][rows, :] = own_ref[rows, :]
        for acc in accs[1:]:
            acc[rows, :] = jnp.zeros((64, columns), jnp.float32)

    chunks(nodes, 64, fill)

    def step(i, carry):
        for u in range(group):
            spots = []
            for o in range(4):
                row = i * group + u + o * slot
                at = pl.ds(targets_ref[row], 1)
                spots.append((accs[o], at, accs[o][at, :] + wide[pl.ds(row, 1), :]))
            for acc, at, value in spots:
                acc[at, :] = value
        return carry

    lax.fori_loop(0, slot // group, step, 0)
    center = (bounds_ref[0] + bounds_ref[1]) * 0.5
    coef = 1.0 / jnp.full((1, columns), (bounds_ref[1] - bounds_ref[0]) * 0.5, jnp.float32)
    size = potential_ref.shape[1]
    turned = potential_ref[...].T - center
    for i in range(nodes // size):
        rows = pl.ds(i * size, size)
        total = (accs[0][rows, :] + accs[1][rows, :]) + (accs[2][rows, :] + accs[3][rows, :])
        level = jnp.broadcast_to(turned[:, i : i + 1], (size, columns))
        image = (total + level * v_ref[rows, :].astype(jnp.float32)) * coef
        if not first:
            image = 2.0 * image - w_ref[rows, :].astype(jnp.float32)
        out_ref[rows, :] = image.astype(jnp.bfloat16)


def combine(first, own, back, v, w, potential, targets, bounds):
    nodes, columns = v.shape
    return pl.pallas_call(
        functools.partial(combine_kernel, first),
        out_shape=jax.ShapeDtypeStruct((nodes, columns), jnp.bfloat16),
        in_specs=[VM, VM, VM, VM, VM, SM, SM],
        out_specs=VM,
        scratch_shapes=[pltpu.VMEM(back.shape, jnp.float32)]
        + [pltpu.VMEM((nodes + 8, columns), jnp.float32)] * 4,
        compiler_params=params(),
        name="combine_one" if first else "combine_two",
    )(own, back, v, w, potential, targets, bounds)


PIECES = 4


def margin_kernel(scaling, x_ref, other_ref, margin_ref, part, slots, send_sem, recv_sem):
    nodes, columns = x_ref.shape
    me = lax.axis_index("dom")
    mine = lax.axis_index("band")
    size = lax.axis_size("dom")
    across = {"band": 1 - mine}
    direct = columns // size >= 8
    if direct:
        peers = [{"dom": lax.rem(me + by, size)} for by in range(1, size)]
    else:
        peers = []
        for k in range(size.bit_length() - 1):
            bit = 1 << k
            peers.append({"dom": me + bit - 2 * bit * (lax.div(me, bit) % 2)})

    barrier = pltpu.get_barrier_semaphore()
    for peer in [across] + peers:
        pl.semaphore_signal(barrier, inc=1, device_id=peer, device_id_type=MESH)
    pl.semaphore_wait(barrier, 1 + len(peers))

    def send(at, src, dst, peer):
        copy = pltpu.make_async_remote_copy(
            src_ref=src,
            dst_ref=dst,
            send_sem=send_sem.at[at],
            recv_sem=recv_sem.at[at],
            device_id=peer,
            device_id_type=MESH,
        )
        copy.start()
        return copy

    chunk = nodes // PIECES
    copies = []
    for c in range(PIECES):
        rows = pl.ds(c * chunk, chunk)
        copies.append(send(c, x_ref.at[rows], other_ref.at[rows], across))
    sums = jnp.zeros((columns, 2 * columns), jnp.float32)
    for c in range(PIECES):
        copies[c].wait()
        rows = pl.ds(c * chunk, chunk)
        own = x_ref[rows, :]
        sums = sums + lax.dot_general(
            own,
            jnp.concatenate([own, other_ref[rows, :]], 1),
            (((0,), (0,)), ((), ())),
            preferred_element_type=jnp.float32,
        )
    sums = sums * scaling
    lanes_mine = pl.ds(pl.multiple_of(mine * columns, columns), columns)
    lanes_other = pl.ds(pl.multiple_of((1 - mine) * columns, columns), columns)
    part[:, lanes_mine] = sums[:, :columns]
    part[:, lanes_other] = sums[:, columns:]
    at = PIECES

    if direct:
        piece = columns // size

        def rows_of(owner):
            return pl.ds(pl.multiple_of(owner * piece, piece), piece)

        def margin_rows(owner):
            return pl.ds(pl.multiple_of(mine * columns + owner * piece, piece), piece)

        copies = []
        for by in range(1, size):
            to = lax.rem(me + by, size)
            copies.append(send(at + by, part.at[rows_of(to)], slots.at[by], peers[by - 1]))
        total = part[rows_of(me), :]
        for by in range(1, size):
            copies[by - 1].wait()
            total = total + slots[by]
        margin_ref[margin_rows(me), :] = total
        at = at + size
        home = margin_ref.at[margin_rows(me)]
        copies = [send(at + by, home, home, peers[by - 1]) for by in range(1, size)]
        at = at + size
        forwards = [send(at, home, home, across)]
        for by in range(1, size):
            copies[by - 1].wait()
            came = margin_ref.at[margin_rows(lax.rem(me + size - by, size))]
            forwards.append(send(at + by, came, came, across))
        for copy in forwards:
            copy.wait()
    else:
        for k, peer in enumerate(peers):
            copy = send(at + k, part, slots.at[k], peer)
            copy.wait()
            part[...] += slots[k]
        margin_ref[lanes_mine, :] = part[...]
        home = margin_ref.at[lanes_mine]
        send(at + len(peers), home, home, across).wait()


def margin_of(x, scaling):
    nodes, columns = x.shape
    size = lax.axis_size("dom")
    direct = columns // size >= 8
    slots = (size, columns // size) if direct else (size.bit_length(), columns)
    copies = PIECES + (3 * size if direct else size.bit_length() + 1)
    return pl.pallas_call(
        functools.partial(margin_kernel, scaling),
        out_shape=(
            jax.ShapeDtypeStruct((nodes, columns), x.dtype),
            jax.ShapeDtypeStruct((2 * columns, 2 * columns), jnp.float32),
        ),
        in_specs=[VM],
        out_specs=(VM, VM),
        scratch_shapes=[
            pltpu.VMEM((columns, 2 * columns), jnp.float32),
            pltpu.VMEM(slots + (2 * columns,), jnp.float32),
            pltpu.SemaphoreType.DMA((copies,)),
            pltpu.SemaphoreType.DMA((copies,)),
        ],
        compiler_params=params(collective_id=3, has_side_effects=True),
        name="margin",
    )(x)


BLOCK = 64


def inverse_factor(block, spread):
    width = 2 * BLOCK
    shape = (8, width)
    count = BLOCK // 8
    lane = lax.broadcasted_iota(jnp.int32, shape, 1)
    sub = lax.broadcasted_iota(jnp.int32, shape, 0)
    doubled = jnp.concatenate([block, block], 1)
    tiles = []
    for t in range(count):
        unit = (lane - BLOCK == sub + 8 * t).astype(jnp.float32)
        tiles.append(jnp.where(lane < BLOCK, doubled[8 * t : 8 * t + 8], unit))
    done = []
    for g in range(count):
        here = spread.at[g % 2]
        for k in range(8):
            here[8 * k : 8 * k + 8, :] = jnp.broadcast_to(tiles[g][:, 8 * g + k : 8 * g + k + 1], shape)
        here[64:72, :] = tiles[g]

        def replicated(at):
            return jnp.broadcast_to(here[at : at + 1, :], shape)

        a = [[replicated(8 * k + i) for k in range(i + 1)] for i in range(8)]
        rows = [replicated(64 + i) for i in range(8)]
        recip = []
        for k in range(8):
            recip.append(1.0 / a[k][k])
            scaled = {i: a[i][k] * recip[k] for i in range(k + 1, 8)}
            for i in range(k + 1, 8):
                for l in range(k + 1, i + 1):
                    a[i][l] = a[i][l] - scaled[i] * a[l][k]
            for i in range(k + 1, 8):
                rows[i] = rows[i] - scaled[i] * rows[k]
                a[i][k] = scaled[i]
        whole = rows[0] * lax.rsqrt(a[0][0])
        for i in range(1, 8):
            whole = jnp.where(sub == i, rows[i] * lax.rsqrt(a[i][i]), whole)
        done.append(whole)
        if g + 1 == count:
            break
        solved = [None] * 8
        for i in range(7, -1, -1):
            value = rows[i] * recip[i]
            for l in range(7, i, -1):
                value = value - a[l][i] * solved[l]
            solved[i] = value
        for t in range(g + 1, count):
            parts = [
                jnp.broadcast_to(tiles[t][:, 8 * g + k : 8 * g + k + 1], shape) * solved[k]
                for k in range(8)
            ]
            while len(parts) > 1:
                parts = [parts[n] + parts[n + 1] for n in range(0, len(parts), 2)]
            tiles[t] = tiles[t] - parts[0]
    return jnp.concatenate(done, 0)[:, BLOCK:]


def finish_kernel(margin_ref, x_ref, other_ref, mine_ref, out_ref, work, spread):
    nodes, columns = x_ref.shape
    bands = margin_ref.shape[0]
    exact = lax.Precision.HIGHEST
    work[...] = margin_ref[...]
    for first in range(0, bands, BLOCK):
        last = first + BLOCK
        inverse = inverse_factor(work[first:last, first:last], spread)
        pieces = [inverse]
        if first:
            pieces = [work[first:last, :first]] + pieces
        if last < bands:
            pieces = pieces + [work[first:last, last:]]
        for at, piece in enumerate(pieces):
            if piece is not inverse:
                pieces[at] = jnp.dot(inverse, piece, precision=exact)
        row = jnp.concatenate(pieces, 1) if len(pieces) > 1 else pieces[0]
        lane = lax.broadcasted_iota(jnp.int32, (BLOCK, bands), 1)
        work[first:last, :] = jnp.where(lane < last, row, 0.0)
        if last < bands:
            update = lax.dot_general(
                row[:, last:], row, (((0,), (0,)), ((), ())), precision=exact
            )
            lane = lax.broadcasted_iota(jnp.int32, (bands - last, bands), 1)
            fresh = jnp.logical_and(lane >= first, lane < last)
            work[last:, :] = jnp.where(fresh, 0.0, work[last:, :]) - update

    mine = mine_ref[0]
    own_at = pl.ds(pl.multiple_of(mine * columns, columns), columns)
    other_at = pl.ds(pl.multiple_of((1 - mine) * columns, columns), columns)
    rows = jnp.concatenate([work[own_at, own_at], work[own_at, other_at]], 1)
    high = rows.astype(jnp.bfloat16)
    low = (rows - high.astype(jnp.float32)).astype(jnp.bfloat16)
    both = jnp.concatenate([high, low], 0)

    def rotate(at):
        panel = jnp.concatenate([x_ref[at, :], other_ref[at, :]], 1)
        value = lax.dot_general(
            panel, both, (((1,), (1,)), ((), ())), preferred_element_type=jnp.float32
        )
        out_ref[at, :] = value[:, :columns] + value[:, columns:]

    chunks(nodes, 512, rotate)


def finish(margin, x, other, mine):
    return pl.pallas_call(
        finish_kernel,
        out_shape=jax.ShapeDtypeStruct(x.shape, jnp.float32),
        in_specs=[VM, VM, VM, SM],
        out_specs=VM,
        scratch_shapes=[
            pltpu.VMEM(margin.shape, jnp.float32),
            pltpu.VMEM((2, 72, 2 * BLOCK), jnp.float32),
        ],
        compiler_params=params(),
        name="finish",
    )(margin, x, other, mine)


def on_device(wavefunctions, bounds, cell_matrix, cell_scale, potential, cell_nodes, face_nodes):
    nodes, columns = wavefunctions.shape
    targets = jnp.where(face_nodes >= 0, face_nodes, nodes).reshape(-1)
    maps = cell_nodes.reshape(-1)
    levels = potential.reshape(nodes // 128, 128)

    def apply_sums(vectors):
        ghosts = exchange_out(vectors, targets)
        own, back = operate(vectors, ghosts, cell_matrix, maps, cell_scale)
        return own, exchange_back(back)

    own, back = apply_sums(wavefunctions)
    one = combine(True, own, back, wavefunctions, wavefunctions, levels, targets, bounds)
    own, back = apply_sums(one)
    two = combine(False, own, back, one, wavefunctions, levels, targets, bounds)
    other, margin = margin_of(two, 1.0 / (nodes * lax.axis_size("dom")))
    return finish(margin, two, other, lax.axis_index("band").reshape(1))


def solution(mesh):
    return jax.shard_map(
        on_device,
        mesh=mesh,
        in_specs=(
            P(("kpt", "dom"), "band"),
            P("kpt"),
            P(),
            P("dom"),
            P("dom"),
            P("dom", None),
            P("dom", None),
        ),
        out_specs=P(("kpt", "dom"), "band"),
        check_vma=False,
    )
```
